32 devices in a mesh: pipe: 4 (over y, core), expert: 8 (over z, x).
Axes of the slice: x: 2, y: 2, z: 4, core: 2. Of those that a mesh axis runs over, the one named last changes fastest.
Arguments:
- forward_input: bfloat16 [4, 1024, 3584], P('pipe', 'expert'), may hold values from -6 to 6
- forward_route: int32 [4, 1024, 1], P('pipe', 'expert'), may hold values from 0 to 1; in each aligned block of 128 rows (0 to 127, 128 to 255, ..., all dimensions but the last counted through in order) at most 96 rows name the same one
- forward_weight: float32 [4, 1024, 1], P('pipe', 'expert'), may hold values from 0.3 to 3
- backward_input: bfloat16 [4, 1024, 3584], P('pipe', 'expert'), may hold values from -6 to 6
- backward_route: int32 [4, 1024, 1], P('pipe', 'expert'), may hold values from 0 to 1; in each aligned block of 128 rows (0 to 127, 128 to 255, ..., all dimensions but the last counted through in order) at most 96 rows name the same one
- backward_weight: float32 [4, 1024, 1], P('pipe', 'expert'), may hold values from 0.3 to 3
- output_grad: bfloat16 [4, 1024, 3584], P('pipe', 'expert'), may hold values from -6 to 6
- norm_gain: float32 [4, 3584], P('pipe'), may hold values from 0.1 to 1.9
- gate_weight: bfloat16 [4, 3584, 2048], P('pipe', None, 'expert'), may hold values from -0.09375 to 0.09375
- up_weight: bfloat16 [4, 3584, 2048], P('pipe', None, 'expert'), may hold values from -0.09375 to 0.09375
- down_weight: bfloat16 [4, 2048, 3584], P('pipe', 'expert'), may hold values from -0.1875 to 0.1875
Outputs:
- next_input: bfloat16 [4, 1024, 3584], P('pipe', 'expert')
- previous_grad: bfloat16 [4, 1024, 3584], P('pipe', 'expert')
The draws below stay inside these ranges and needn't reach their ends.
Inputs may be any that keep to these rules, and one draw needn't show every extreme that they name: `forward_route`: each token is routed to exactly one expert. Among the 128 tokens of one device no expert is named more than 96 times, and in some device's tokens one expert is named exactly 96 times. `backward_route`: as forward_route.
All inputs are finite; a program needn't handle non-finite values.
Results may differ from the reference program's by a relative error of at most 0.0066.
Values may be sent and summed in bfloat16 or wider, within the bound.
A program may use at most 192 MiB of HBM per device.

```python
import math
import jax
import jax.numpy as jnp
import numpy as np
from jax import lax

D = 3584
HID = 1024
HD = 256
TOP = 1
TOK = 128
EXPERTS = 2
CAP = 96
TOKENS = 1024
N_PIPE = 4
N_EXPERT = 8


def levels(own_key, extent, cuts, least, high):
    loudness, own = 1.0, jax.random.fold_in(own_key, 6)
    for dim, blocks in cuts:
        draws = jnp.exp(jax.random.uniform(jax.random.fold_in(own, dim), (blocks,), jnp.float32, least / len(cuts), high / len(cuts)))
        loudness = loudness * jnp.repeat(draws, extent[dim] // blocks).reshape([-1 if axis == dim else 1 for axis in range(len(extent))])
    return loudness


def routed_block(stream_key, own, number, rows, amount, top, most, lean):
    order = jax.random.permutation(stream_key, amount)
    crowded, ordinary = load_shares(amount, rows * top, most, lean, True), load_shares(amount, rows * top, most, lean, False)
    places = jnp.arange(amount)

    def named(lengths, turn):
        used = int((lengths > 0).sum())
        fixed = max(1, used // 4)
        shifted = fixed + (places - fixed + turn * (used - fixed)) % max(1, amount - fixed)
        return jnp.zeros((amount,), jnp.int32).at[order[jnp.where(places < fixed, places, shifted)]].set(jnp.asarray(lengths, jnp.int32))

    lengths = jnp.where(number % 4 == 0, named(crowded, number // 4), named(ordinary, number - number // 4 - 1))
    mixed = jax.random.permutation(jax.random.fold_in(own, 3), amount)
    donor, receiver = mixed[0:amount // 2 * 2:2], mixed[1:amount // 2 * 2:2]
    room = jnp.minimum(lengths[donor] - 1, most - lengths[receiver]) // 2
    room = jnp.where((donor == order[0]) | (receiver == order[0]) | (lengths[receiver] == 0), 0, jnp.maximum(room, 0))
    shifted = jax.random.randint(jax.random.fold_in(own, 4), (amount // 2,), 0, 1 << 20) % (room + 1)
    lengths = lengths.at[donor].add(-shifted).at[receiver].add(shifted)
    items = jnp.searchsorted(jnp.cumsum(lengths), jnp.arange(rows * top), side="right").astype(jnp.int32)
    table = items.reshape(top, rows).T
    table = table[jax.random.permutation(jax.random.fold_in(own, 1), rows)]
    turn = jax.random.randint(jax.random.fold_in(own, 2), (rows, 1), 0, top)
    return jnp.take_along_axis(table, (jnp.arange(top)[None, :] + turn) % top, axis=1)


def load_shares(number_of, total, most, lean, full):
    weights = [(1 << 20) // math.isqrt(grade ** lean) + 1 for grade in range(1, number_of + 1)]
    largest = most if full else min(most, max(-(-total // number_of), total * weights[0] // sum(weights)))
    least = 1 if total - largest >= number_of - 1 else 0
    holding, rest = [largest] + [least] * (number_of - 1), total - largest - least * (number_of - 1)
    while rest > 0:
        free = [i for i in range(1, number_of) if holding[i] < largest] or [i for i in range(1, number_of) if holding[i] < most]
        mass, left = sum([weights[i] for i in free]), rest
        for i in free:
            extra = min(most - holding[i], max(1, left * weights[i] // mass), rest)
            holding[i] = holding[i] + extra
            rest = rest - extra
    return np.array(holding)


def noise(rng, extent, scale, reach, cuts=(), kind=jnp.bfloat16):
    entries = jax.random.normal(rng, extent, jnp.float32) * scale
    if len(cuts) > 0:
        entries = levels(rng, extent, cuts, -0.22, 0.18) * entries
    return jnp.clip(entries, min=-reach, max=reach).astype(kind)


def setup_inputs(seed: int = 0) -> dict:
    streams_of = jax.random.split(jax.random.key(seed), 12)
    forward_input = noise(streams_of[0], (N_PIPE, TOKENS, D), 1.0, 6.0, ((0, 4), (1, 8)))
    forward_route_keys = jax.random.split(jax.random.fold_in(streams_of[1], 1), N_PIPE * TOKENS // TOK)
    forward_route_turns = jax.random.permutation(jax.random.fold_in(streams_of[1], 3), N_PIPE * TOKENS // TOK)
    forward_route = jax.vmap(lambda own, number: routed_block(jax.random.fold_in(streams_of[1], 2), own, number, TOK, EXPERTS, TOP, CAP, 2))(forward_route_keys, forward_route_turns).reshape((N_PIPE, TOKENS, TOP))
    forward_weight = jnp.clip(jnp.exp(math.log(3.0) - 2.3025851 * jax.random.uniform(streams_of[2], (N_PIPE, TOKENS, TOP), jnp.float32) ** levels(streams_of[2], (N_PIPE, TOKENS, TOP), ((0, 4), (1, 8)), -0.2, 0.2)), 0.3, 3.0)
    backward_input = noise(streams_of[3], (N_PIPE, TOKENS, D), 1.0, 6.0, ((0, 4), (1, 8)))
    backward_route_keys = jax.random.split(jax.random.fold_in(streams_of[4], 1), N_PIPE * TOKENS // TOK)
    backward_route_turns = jax.random.permutation(jax.random.fold_in(streams_of[4], 3), N_PIPE * TOKENS // TOK)
    backward_route = jax.vmap(lambda own, number: routed_block(jax.random.fold_in(streams_of[4], 2), own, number, TOK, EXPERTS, TOP, CAP, 2))(backward_route_keys, backward_route_turns).reshape((N_PIPE, TOKENS, TOP))
    backward_weight = jnp.clip(jnp.exp(math.log(3.0) - 2.3025851 * jax.random.uniform(streams_of[5], (N_PIPE, TOKENS, TOP), jnp.float32) ** levels(streams_of[5], (N_PIPE, TOKENS, TOP), ((0, 4), (1, 8)), -0.2, 0.2)), 0.3, 3.0)
    output_grad = noise(streams_of[6], (N_PIPE, TOKENS, D), 1.0, 6.0, ((0, 4), (1, 8)))
    norm_gain = jnp.clip(1.0 + 0.18 * jax.random.normal(streams_of[7], (N_PIPE, D), jnp.float32), 0.1, 1.9)
    gate_weight = noise(streams_of[8], (N_PIPE, D, EXPERTS * HID), D ** -0.5, 0.09375, ((0, 4), (2, 8)))
    up_weight = noise(streams_of[9], (N_PIPE, D, EXPERTS * HID), D ** -0.5, 0.09375, ((0, 4), (2, 8)))
    down_weight = noise(streams_of[10], (N_PIPE, EXPERTS * HID, D), HID ** -0.5, 0.1875, ((0, 4), (1, 8)))
    return dict(forward_input=forward_input, forward_route=forward_route, forward_weight=forward_weight, backward_input=backward_input, backward_route=backward_route, backward_weight=backward_weight, output_grad=output_grad, norm_gain=norm_gain, gate_weight=gate_weight, up_weight=up_weight, down_weight=down_weight)


EPS = 1e-06

def normalize(values, gain):
    widened = values.astype(jnp.float32)
    scale = lax.rsqrt(lax.optimization_barrier(jnp.mean(widened * widened, axis=-1, keepdims=True)) + EPS)
    return (widened, scale, (widened * scale * gain).astype(jnp.bfloat16))

def rounded_sum(terms):
    return lax.optimization_barrier(jnp.sum(lax.optimization_barrier(terms.astype(jnp.bfloat16)).astype(jnp.float32), axis=1))

def one_section(inputs):
    forward_input, forward_route, forward_weight, backward_input, backward_route, backward_weight, output_grad, norm_gain, gate_weight, up_weight, down_weight = inputs
    blocks = HID // HD
    limit = N_EXPERT * CAP
    pairs = TOKENS * TOP
    ahead_wide, ahead_scale, ahead_normed = normalize(forward_input, norm_gain)
    behind_wide, behind_scale, behind_normed = normalize(backward_input, norm_gain)
    zero_row = jnp.zeros((1, D), jnp.bfloat16)
    ahead_table = jnp.concatenate([ahead_normed, zero_row], axis=0)
    behind_table = jnp.concatenate([behind_normed, zero_row], axis=0)
    cotangent = output_grad.astype(jnp.float32)
    routed_grad = (jnp.repeat(cotangent, TOP, axis=0) * backward_weight.reshape(-1)[:, None]).astype(jnp.bfloat16)
    grad_table = jnp.concatenate([routed_grad, zero_row], axis=0)
    ahead_routes = forward_route.reshape(-1)
    behind_routes = backward_route.reshape(-1)

    def per_expert(carry, expert):
        ahead_values, behind_values = carry
        ahead_index = jnp.nonzero(ahead_routes == expert, size=limit, fill_value=pairs)[0].astype(jnp.int32)
        behind_index = jnp.nonzero(behind_routes == expert, size=limit, fill_value=pairs)[0].astype(jnp.int32)
        start = (expert * HID).astype(jnp.int32)
        gate_cols = lax.dynamic_slice_in_dim(gate_weight, start, HID, 1)
        up_cols = lax.dynamic_slice_in_dim(up_weight, start, HID, 1)
        down_rows = lax.dynamic_slice_in_dim(down_weight, start, HID, 0)
        down_blocks = down_rows.astype(jnp.float32).reshape(blocks, HD, D)
        gate_blocks = gate_cols.astype(jnp.float32).reshape(D, blocks, HD)
        up_blocks = up_cols.astype(jnp.float32).reshape(D, blocks, HD)
        chosen = ahead_table[ahead_index // TOP]
        gate_pre = jnp.dot(chosen, gate_cols, preferred_element_type=jnp.float32)
        up_pre = jnp.dot(chosen, up_cols, preferred_element_type=jnp.float32)
        hidden = (jax.nn.silu(gate_pre) * up_pre).astype(jnp.bfloat16)
        parts = jnp.einsum('rgk,gkd->rgd', hidden.astype(jnp.float32).reshape(limit, blocks, HD), down_blocks)
        ahead_values = ahead_values.at[ahead_index].set(rounded_sum(parts), mode='drop')
        picked = behind_table[behind_index // TOP]
        grads = grad_table[behind_index]
        gate_back = jnp.dot(picked, gate_cols, preferred_element_type=jnp.float32)
        up_back = jnp.dot(picked, up_cols, preferred_element_type=jnp.float32)
        hidden_grad = jnp.dot(grads, down_rows.T, preferred_element_type=jnp.float32)
        sigmoid_gate = jax.nn.sigmoid(gate_back)
        gate_grad = (hidden_grad * up_back * sigmoid_gate * (1.0 + gate_back * (1.0 - sigmoid_gate))).astype(jnp.bfloat16)
        up_grad = (hidden_grad * gate_back * sigmoid_gate).astype(jnp.bfloat16)
        back = jnp.einsum('rgk,dgk->rgd', gate_grad.astype(jnp.float32).reshape(limit, blocks, HD), gate_blocks)
        back = back + jnp.einsum('rgk,dgk->rgd', up_grad.astype(jnp.float32).reshape(limit, blocks, HD), up_blocks)
        behind_values = behind_values.at[behind_index].set(rounded_sum(back), mode='drop')
        return ((ahead_values, behind_values), None)
    start_values = (jnp.zeros((pairs, D), jnp.float32), jnp.zeros((pairs, D), jnp.float32))
    (ahead_values, behind_values), _ = lax.scan(per_expert, start_values, jnp.arange(EXPERTS, dtype=jnp.int32))
    mixed = lax.optimization_barrier(jnp.sum(ahead_values.reshape(TOKENS, TOP, D) * forward_weight[:, :, None], axis=1))
    section_out = (ahead_wide + mixed).astype(jnp.bfloat16)
    normed_grad = lax.optimization_barrier(jnp.sum(behind_values.reshape(TOKENS, TOP, D), axis=1))
    unit = behind_wide * behind_scale
    unit_grad = norm_gain * normed_grad
    section_grad = cotangent + behind_scale * (unit_grad - unit * lax.optimization_barrier(jnp.mean(unit_grad * unit, axis=-1, keepdims=True)))
    return (section_out, section_grad.astype(jnp.bfloat16))

def reference(forward_input, forward_route, forward_weight, backward_input, backward_route, backward_weight, output_grad, norm_gain, gate_weight, up_weight, down_weight):
    section_out, section_grad = lax.map(one_section, (forward_input, forward_route, forward_weight, backward_input, backward_route, backward_weight, output_grad, norm_gain, gate_weight, up_weight, down_weight))
    return (jnp.roll(section_out, 1, axis=0), jnp.roll(section_grad, -1, axis=0))
```

```python
import jax
import jax.numpy as jnp
from jax import lax
from jax.sharding import PartitionSpec as P

HID = 1024


EPS = 1e-06


def passed_along(array, axis, by):
    devices = lax.axis_size(axis)
    return lax.ppermute(array, axis, [(i, (i + by) % devices) for i in range(devices)])


def swapped(array, bit):
    devices = lax.axis_size("expert")
    return lax.ppermute(array, "expert", [(i, i ^ bit) for i in range(devices)])


def normalize(values, gain):
    widened = values.astype(jnp.float32)
    scale = lax.rsqrt(jnp.mean(widened * widened, axis=-1, keepdims=True) + EPS)
    return (widened, scale, (widened * scale * gain).astype(jnp.bfloat16))


def slot_matrix(routes, experts, capacity, mine):
    flat = lax.rem(routes.reshape(-1) + (experts - mine), experts)
    pairs = flat.shape[0]
    onehot = flat[:, None] == jnp.arange(experts, dtype=jnp.int32)[None, :]
    before = jnp.arange(pairs)[:, None] > jnp.arange(pairs)[None, :]
    counts = jnp.dot(
        before.astype(jnp.bfloat16), onehot.astype(jnp.bfloat16), preferred_element_type=jnp.float32
    )
    ranks = jnp.sum(jnp.where(onehot, counts, 0.0), axis=1).astype(jnp.int32)
    target = flat * capacity + ranks
    slots = jnp.arange(experts * capacity, dtype=jnp.int32)
    return (slots[:, None] == target[None, :]).astype(jnp.bfloat16)


def to_slots(matrix, rows):
    return jnp.dot(matrix, rows, preferred_element_type=jnp.float32).astype(jnp.bfloat16)


def from_slots(matrix, rows):
    return lax.dot_general(
        matrix, rows, (((0,), (0,)), ((), ())), preferred_element_type=jnp.float32
    )


def across(slots, experts, group, sign):
    blocks = jnp.split(slots, experts, axis=0)
    return blocks[:1] + [
        passed_along(blocks[k], "expert", sign * group * k) for k in range(1, experts)
    ]


def dot(a, b):
    return jnp.dot(a, b, preferred_element_type=jnp.float32)


def dot_t(a, b):
    return lax.dot_general(a, b, (((1,), (1,)), ((), ())), preferred_element_type=jnp.float32)


def forward_sum(rows, weights):
    total = None
    for gate, up, down in weights:
        hidden = (jax.nn.silu(dot(rows, gate)) * dot(rows, up)).astype(jnp.bfloat16)
        part = dot(hidden, down)
        total = part if total is None else total + part
    return total


def backward_sum(rows, grads, weights):
    total = None
    for gate, up, down in weights:
        gate_back = dot(rows, gate)
        up_back = dot(rows, up)
        hidden_grad = dot_t(grads, down)
        sig = jax.nn.sigmoid(gate_back)
        gate_grad = (hidden_grad * up_back * sig * (1.0 + gate_back * (1.0 - sig))).astype(
            jnp.bfloat16
        )
        up_grad = (hidden_grad * gate_back * sig).astype(jnp.bfloat16)
        part = dot_t(gate_grad, gate) + dot_t(up_grad, up)
        total = part if total is None else total + part
    return total


def per_device(
    forward_input,
    forward_route,
    forward_weight,
    backward_input,
    backward_route,
    backward_weight,
    output_grad,
    norm_gain,
    gate_weight,
    up_weight,
    down_weight,
):
    group = HID // gate_weight.shape[2]
    assert group == 4
    experts = lax.axis_size("expert") // group
    tokens = forward_input.shape[1]
    top = forward_route.shape[2]
    width = forward_input.shape[2]
    capacity = max(2, 3 * tokens * top // (2 * experts))
    mine = lax.axis_index("expert") // group
    gain = norm_gain[0]
    own = (gate_weight[0], up_weight[0], down_weight[0])
    other = tuple(swapped(w, 2) for w in own)
    weights = (own, other)

    ahead_wide, ahead_scale, ahead_normed = normalize(forward_input[0], gain)
    behind_wide, behind_scale, behind_normed = normalize(backward_input[0], gain)
    cotangent = output_grad[0].astype(jnp.float32)
    routed_grad = (
        jnp.repeat(cotangent, top, axis=0) * backward_weight[0].reshape(-1)[:, None]
    ).astype(jnp.bfloat16)
    ahead_slots = slot_matrix(forward_route[0], experts, capacity, mine)
    behind_slots = slot_matrix(backward_route[0], experts, capacity, mine)

    def gathered(matrix, rows):
        pieces = across(to_slots(matrix, rows), experts, group, 1)
        near = jnp.concatenate(pieces, axis=0)
        far = jnp.concatenate(
            [swapped(pieces[0], 1), swapped(jnp.concatenate(pieces[1:], axis=0), 1)], axis=0
        )
        return near, far

    def returned(near_sum, far_sum):
        total = (near_sum + swapped(far_sum.astype(jnp.bfloat16), 1)).astype(jnp.bfloat16)
        return jnp.concatenate(across(total, experts, group, -1), axis=0)

    ahead_near, ahead_far = gathered(ahead_slots, jnp.repeat(ahead_normed, top, axis=0))
    behind_near, behind_far = gathered(behind_slots, jnp.repeat(behind_normed, top, axis=0))
    grad_near, grad_far = gathered(behind_slots, routed_grad)

    ahead_back = returned(forward_sum(ahead_near, weights), forward_sum(ahead_far, weights))
    ahead_values = from_slots(ahead_slots, ahead_back)
    mixed = jnp.sum(
        ahead_values.reshape(tokens, top, width) * forward_weight[0][:, :, None], axis=1
    )
    section_out = (ahead_wide + mixed).astype(jnp.bfloat16)
    next_input = passed_along(section_out, "pipe", 1)

    behind_back = returned(
        backward_sum(behind_near, grad_near, weights), backward_sum(behind_far, grad_far, weights)
    )
    behind_values = from_slots(behind_slots, behind_back)
    normed_grad = jnp.sum(behind_values.reshape(tokens, top, width), axis=1)
    unit = behind_wide * behind_scale
    unit_grad = gain * normed_grad
    section_grad = cotangent + behind_scale * (
        unit_grad - unit * jnp.mean(unit_grad * unit, axis=-1, keepdims=True)
    )
    section_grad = section_grad.astype(jnp.bfloat16)
    previous_grad = passed_along(section_grad, "pipe", -1)
    return (next_input[None], previous_grad[None])


def solution(mesh):
    return jax.shard_map(
        per_device,
        mesh=mesh,
        in_specs=(
            P("pipe", "expert", None),
            P("pipe", "expert", None),
            P("pipe", "expert", None),
            P("pipe", "expert", None),
            P("pipe", "expert", None),
            P("pipe", "expert", None),
            P("pipe", "expert", None),
            P("pipe", None),
            P("pipe", None, "expert"),
            P("pipe", None, "expert"),
            P("pipe", "expert", None),
        ),
        out_specs=(P("pipe", "expert", None), P("pipe", "expert", None)),
        check_vma=False,
    )
```

```python
import functools

import jax
import jax.numpy as jnp
from jax import lax
from jax.experimental import pallas as pl
from jax.experimental.pallas import tpu as pltpu
from jax.sharding import PartitionSpec as P

HID = 1024


EPS = 1e-06


def passed_along(array, axis, by):
    devices = lax.axis_size(axis)
    return lax.ppermute(array, axis, [(i, (i + by) % devices) for i in range(devices)])


def swapped(array, bit):
    devices = lax.axis_size("expert")
    return lax.ppermute(array, "expert", [(i, i ^ bit) for i in range(devices)])


def normalize(values, gain):
    widened = values.astype(jnp.float32)
    scale = lax.rsqrt(jnp.mean(widened * widened, axis=-1, keepdims=True) + EPS)
    return (widened, scale, (widened * scale * gain).astype(jnp.bfloat16))


def slot_matrix(routes, experts, capacity, mine):
    flat = lax.rem(routes.reshape(-1) + (experts - mine), experts)
    pairs = flat.shape[0]
    onehot = flat[:, None] == jnp.arange(experts, dtype=jnp.int32)[None, :]
    before = jnp.arange(pairs)[:, None] > jnp.arange(pairs)[None, :]
    counts = jnp.dot(
        before.astype(jnp.bfloat16), onehot.astype(jnp.bfloat16), preferred_element_type=jnp.float32
    )
    ranks = jnp.sum(jnp.where(onehot, counts, 0.0), axis=1).astype(jnp.int32)
    target = flat * capacity + ranks
    slots = jnp.arange(experts * capacity, dtype=jnp.int32)
    return (slots[:, None] == target[None, :]).astype(jnp.bfloat16)


def to_slots(matrix, rows):
    return jnp.dot(matrix, rows, preferred_element_type=jnp.float32).astype(jnp.bfloat16)


def from_slots(matrix, rows):
    return lax.dot_general(
        matrix, rows, (((0,), (0,)), ((), ())), preferred_element_type=jnp.float32
    )


def across(slots, experts, group, sign):
    blocks = jnp.split(slots, experts, axis=0)
    return blocks[:1] + [
        passed_along(blocks[k], "expert", sign * group * k) for k in range(1, experts)
    ]


def dot(a, b):
    return jnp.dot(a, b, preferred_element_type=jnp.float32)


def dot_t(a, b):
    return lax.dot_general(a, b, (((1,), (1,)), ((), ())), preferred_element_type=jnp.float32)


def forward_sum(rows, weights):
    total = None
    for gate, up, down in weights:
        hidden = (jax.nn.silu(dot(rows, gate)) * dot(rows, up)).astype(jnp.bfloat16)
        part = dot(hidden, down)
        total = part if total is None else total + part
    return total


def backward_sum(rows, grads, weights):
    total = None
    for gate, up, down in weights:
        gate_back = dot(rows, gate)
        up_back = dot(rows, up)
        hidden_grad = dot_t(grads, down)
        sig = jax.nn.sigmoid(gate_back)
        gate_grad = (hidden_grad * up_back * sig * (1.0 + gate_back * (1.0 - sig))).astype(
            jnp.bfloat16
        )
        up_grad = (hidden_grad * gate_back * sig).astype(jnp.bfloat16)
        part = dot_t(gate_grad, gate) + dot_t(up_grad, up)
        total = part if total is None else total + part
    return total


MESH = pl.DeviceIdType.MESH
BF = jnp.bfloat16
F32 = jnp.float32


def slot_targets(routes, experts, capacity, mine):
    flat = lax.rem(routes.reshape(-1) + (experts - mine), experts)
    pairs = flat.shape[0]
    onehot = flat[:, None] == jnp.arange(experts, dtype=jnp.int32)[None, :]
    before = jnp.arange(pairs)[:, None] > jnp.arange(pairs)[None, :]
    counts = dot(before.astype(BF), onehot.astype(BF))
    ranks = jnp.sum(jnp.where(onehot, counts, 0.0), axis=1).astype(jnp.int32)
    return flat * capacity + ranks


def section_kernel(
    cfg,
    fx, bx, og, gain, fw, bw, s_f, s_b, st_f, st_b, gate, up, down,
    next_ref, prev_ref,
    g0, u0, g1, u1, dd, rows_f, rows_b, rows_g, out_f, out_b, out_g,
    acc_a, acc_b, acc_c, hid, ggr, ugr, far_f, far_b, x_f, x_b, back_f, back_b,
    ret_f, ret_b, ngr, fin_f, fin_b, tmp, scale_b,
    w_sem, wl_sem, in_s, in_r, xl_s, xl_r, xf_s, xf_r, xo_s, xo_r, re_s, re_r, pi_s, pi_r,
):
    experts, group, cap, chunks, cw = cfg
    tokens, width = fx.shape
    rows = experts * cap
    hd = gate.shape[1]
    n = experts * group
    me = lax.axis_index("expert")
    pipe = lax.axis_index("pipe")
    pipes = lax.axis_size("pipe")
    xp = me + 1 - 2 * lax.rem(me, 2)
    zp = me + 2 - 4 * lax.rem(lax.div(me, 2), 2)
    onward = {"pipe": lax.rem(pipe + 1, pipes)}
    behind = {"pipe": lax.rem(pipe + pipes - 1, pipes)}

    def ahead_of(k):
        return {"expert": lax.rem(me + group * k, n)}

    def back_of(k):
        return {"expert": lax.rem(me + n - group * k, n)}

    def remote(src, dst, ss, rs, dev):
        return pltpu.make_async_remote_copy(
            src_ref=src, dst_ref=dst, send_sem=ss, recv_sem=rs, device_id=dev, device_id_type=MESH
        )

    barrier = pltpu.get_barrier_semaphore()
    peers = [ahead_of(k) for k in range(1, experts)]
    peers += [{"expert": xp}, {"expert": zp}, onward, behind]
    for peer in peers:
        pl.semaphore_signal(barrier, inc=1, device_id=peer, device_id_type=MESH)
    pl.semaphore_wait(barrier, len(peers))

    heavy = [
        remote(src, dst, w_sem.at[0, i], w_sem.at[1, i], {"expert": zp})
        for i, (src, dst) in enumerate(((gate, g1), (up, u1), (down, dd.at[pl.ds(hd, hd)])))
    ]
    local = [
        pltpu.make_async_copy(src, dst, wl_sem.at[i])
        for i, (src, dst) in enumerate(((gate, g0), (up, u0), (down, dd.at[pl.ds(0, hd)])))
    ]

    def col(c):
        return pl.ds(pl.multiple_of(c * cw, cw), cw)

    def each_chunk(body):
        def step(c, carry):
            body(c)
            return carry

        lax.fori_loop(0, chunks, step, 0)

    def each_band(body):
        def step(i, carry):
            body(pl.ds(pl.multiple_of(i * 16, 16), 16))
            return carry

        lax.fori_loop(0, tokens // 16, step, 0)

    def norm_into(src, keep):
        def body(band):
            wide = src[band, :].astype(F32)
            scale = lax.rsqrt(jnp.mean(wide * wide, axis=-1, keepdims=True) + EPS)
            tmp[band, :] = (wide * scale * gain[...]).astype(BF)
            if keep is not None:
                keep[band, :] = scale

        each_band(body)

    def weigh_into():
        def body(band):
            tmp[band, :] = (og[band, :].astype(F32) * bw[band, :]).astype(BF)

        each_band(body)

    def crossing(a, out, into):
        return [
            remote(
                out.at[pl.ds((k - 1) * cap, cap)],
                into.at[pl.ds(k * cap, cap)],
                in_s.at[a, k - 1],
                in_r.at[a, k - 1],
                ahead_of(k),
            )
            for k in range(1, experts)
        ]

    def near_x(a, into):
        return remote(
            into.at[pl.ds(0, cap)], into.at[pl.ds(rows, cap)], xl_s.at[a], xl_r.at[a], {"expert": xp}
        )

    def far_x(a, into):
        return remote(
            into.at[pl.ds(cap, rows - cap)],
            into.at[pl.ds(rows + cap, rows - cap)],
            xf_s.at[a],
            xf_r.at[a],
            {"expert": xp},
        )

    def place(matrix, out, into):
        def body(c):
            picked = dot(matrix[...], tmp[:, col(c)]).astype(BF)
            into[pl.ds(0, cap), col(c)] = picked[:cap]
            out[:, col(c)] = picked[cap:]

        each_chunk(body)

    sets = ((s_f, out_f, rows_f), (s_b, out_b, rows_b), (s_b, out_g, rows_g))
    pending = []
    crossings, nears, fars = [], [], []
    for a, (matrix, out, into) in enumerate(sets):
        if a == 0:
            norm_into(fx, None)
        elif a == 1:
            norm_into(bx, scale_b)
        else:
            weigh_into()
        place(matrix, out, into)
        cross = crossing(a, out, into)
        for copy in cross:
            copy.start()
        near = near_x(a, into)
        near.start()
        crossings.append(cross)
        nears.append(near)
        pending += cross + [near]
        if a == 0:
            for copy in heavy + local:
                copy.start()
            pending += heavy

    for a in range(3):
        for copy in crossings[a]:
            copy.wait_recv()
        far = far_x(a, sets[a][2])
        far.start()
        fars.append(far)
        pending.append(far)
    for copy in local:
        copy.wait()

    def first(source, weight, acc):
        acc[...] = jnp.zeros_like(acc)

        def body(c):
            acc[...] += dot(source[:, col(c)], weight[col(c), :])

        each_chunk(body)

    def first_t(source, half, acc):
        acc[...] = jnp.zeros_like(acc)

        def body(c):
            acc[...] += dot_t(source[:, col(c)], dd[pl.ds(half * hd, hd), col(c)])

        each_chunk(body)

    def hidden_half(half, gw, uw):
        first(rows_f, gw, acc_a)
        first(rows_f, uw, acc_b)
        pre = acc_a[...]
        hid[:, pl.ds(half * hd, hd)] = (pre * jax.nn.sigmoid(pre) * acc_b[...]).astype(BF)

    def grads_half(half, gw, uw):
        first(rows_b, gw, acc_a)
        first(rows_b, uw, acc_b)
        first_t(rows_g, half, acc_c)
        pre, upb, hg = acc_a[...], acc_b[...], acc_c[...]
        sig = jax.nn.sigmoid(pre)
        ggr[:, pl.ds(half * hd, hd)] = (hg * upb * sig * (1.0 + pre * (1.0 - sig))).astype(BF)
        ugr[:, pl.ds(half * hd, hd)] = (hg * pre * sig).astype(BF)

    nears[0].wait_recv()
    fars[0].wait_recv()
    hidden_half(0, g0, u0)
    for a in (1, 2):
        nears[a].wait_recv()
        fars[a].wait_recv()
    grads_half(0, g0, u0)
    for copy in heavy:
        copy.wait_recv()
    hidden_half(1, g1, u1)

    def sum_f(at, c):
        return dot(hid[pl.ds(at, rows), :], dd[:, col(c)])

    def sum_b(at, c):
        ga, ua = ggr[pl.ds(at, rows), :], ugr[pl.ds(at, rows), :]
        total = dot_t(ga[:, :hd], g0[col(c), :]) + dot_t(ga[:, hd:], g1[col(c), :])
        return total + dot_t(ua[:, :hd], u0[col(c), :]) + dot_t(ua[:, hd:], u1[col(c), :])

    def x_out(a, c):
        src, dst = ((far_f, x_f), (far_b, x_b))[a]
        return remote(src.at[c], dst.at[c], xo_s.at[a, c], xo_r.at[a, c], {"expert": xp})

    def going_back(a, c):
        src, dst = ((ret_f, back_f), (ret_b, back_b))[a]
        return [
            remote(
                src.at[c, pl.ds((k - 1) * cap, cap)],
                dst.at[c, pl.ds(k * cap, cap)],
                re_s.at[a, c, k - 1],
                re_r.at[a, c, k - 1],
                back_of(k),
            )
            for k in range(1, experts)
        ]

    def leaving(a, c):
        src, dst, dev = ((fin_f, next_ref, onward), (fin_b, prev_ref, behind))[a]
        return remote(src.at[c], dst.at[:, col(c)], pi_s.at[a, c], pi_r.at[a, c], dev)

    def far_step_f(c):
        far_f[c] = sum_f(rows, c).astype(BF)
        x_out(0, c).start()

    each_chunk(far_step_f)
    grads_half(1, g1, u1)

    def far_step_b(c):
        far_b[c] = sum_b(rows, c).astype(BF)

    each_chunk(far_step_b)

    def near_step(a, summed, x_in, back, ret):
        def body(c):
            total = summed(0, c)
            x_out(a, c).wait_recv()
            total = (total + x_in[c].astype(F32)).astype(BF)
            back[c, pl.ds(0, cap), :] = total[:cap]
            ret[c] = total[cap:]
            for copy in going_back(a, c):
                copy.start()

        return body

    each_chunk(near_step(0, sum_f, x_f, back_f, ret_f))

    def start_b(c):
        x_out(1, c).start()

    each_chunk(start_b)
    each_chunk(near_step(1, sum_b, x_b, back_b, ret_b))

    def final_f(c):
        for copy in going_back(0, c):
            copy.wait_recv()
        values = dot(st_f[...], back_f[c])
        fin_f[c] = (fx[:, col(c)].astype(F32) + fw[...] * values).astype(BF)
        leaving(0, c).start()

    each_chunk(final_f)

    def gather_b(c, carry):
        for copy in going_back(1, c):
            copy.wait_recv()
        unit_grad = gain[:, col(c)] * dot(st_b[...], back_b[c])
        ngr[c] = unit_grad
        unit = bx[:, col(c)].astype(F32) * scale_b[...]
        return carry + jnp.sum(unit_grad * unit, axis=-1, keepdims=True)

    mean = lax.fori_loop(0, chunks, gather_b, jnp.zeros((tokens, 1), F32)) / width

    def final_b(c):
        unit = bx[:, col(c)].astype(F32) * scale_b[...]
        grad = og[:, col(c)].astype(F32) + scale_b[...] * (ngr[c] - unit * mean)
        fin_b[c] = grad.astype(BF)
        leaving(1, c).start()

    each_chunk(final_b)

    for copy in pending:
        copy.wait_send()

    def drain(c):
        for a in range(2):
            x_out(a, c).wait_send()
            for copy in going_back(a, c):
                copy.wait_send()
            leaving(a, c).wait()

    each_chunk(drain)


def fused(fi, fr, fwt, bi, br, bwt, og, gain, gate, up, down, experts, group, cap):
    tokens, width = fi.shape
    hd = gate.shape[1]
    rows = experts * cap
    cw = 512
    chunks = width // cw
    mine = lax.axis_index("expert") // group
    slots = jnp.arange(rows, dtype=jnp.int32)
    t_f = slot_targets(fr, experts, cap, mine)
    t_b = slot_targets(br, experts, cap, mine)
    s_f, s_b = [(slots[:, None] == t[None, :]).astype(BF) for t in (t_f, t_b)]
    st_f, st_b = [(t[:, None] == slots[None, :]).astype(BF) for t in (t_f, t_b)]
    vm = pltpu.VMEM
    sem = pltpu.SemaphoreType.DMA
    others = experts - 1
    scratch = [vm((width, hd), BF)] * 4 + [vm((2 * hd, width), BF)]
    scratch += [vm((2 * rows, width), BF)] * 3 + [vm((others * cap, width), BF)] * 3
    scratch += [vm((2 * rows, hd), F32)] * 3 + [vm((2 * rows, 2 * hd), BF)] * 3
    scratch += [vm((chunks, rows, cw), BF)] * 6 + [vm((chunks, others * cap, cw), BF)] * 2
    scratch += [vm((chunks, tokens, cw), F32)] + [vm((chunks, tokens, cw), BF)] * 2
    scratch += [vm((tokens, width), BF), vm((tokens, 1), F32)]
    scratch += [sem((2, 3)), sem((3,)), sem((3, others)), sem((3, others))]
    scratch += [sem((3,))] * 4 + [sem((2, chunks))] * 2
    scratch += [sem((2, chunks, others))] * 2 + [sem((2, chunks))] * 2
    out = jax.ShapeDtypeStruct((tokens, width), BF)
    anywhere = pl.BlockSpec(memory_space=pl.ANY)
    return pl.pallas_call(
        functools.partial(section_kernel, (experts, group, cap, chunks, cw)),
        out_shape=(out, out),
        in_specs=[pl.BlockSpec(memory_space=vm)] * 10 + [anywhere] * 3,
        out_specs=(anywhere, anywhere),
        scratch_shapes=scratch,
        compiler_params=pltpu.CompilerParams(
            collective_id=0, has_side_effects=True, vmem_limit_bytes=58 * 1024 * 1024
        ),
    )(fi, bi, og, gain, fwt, bwt, s_f, s_b, st_f, st_b, gate, up, down)


def per_device(
    forward_input,
    forward_route,
    forward_weight,
    backward_input,
    backward_route,
    backward_weight,
    output_grad,
    norm_gain,
    gate_weight,
    up_weight,
    down_weight,
):
    group = HID // gate_weight.shape[2]
    assert group == 4
    experts = lax.axis_size("expert") // group
    tokens = forward_input.shape[1]
    top = forward_route.shape[2]
    width = forward_input.shape[2]
    capacity = max(2, 3 * tokens * top // (2 * experts))
    if top == 1 and capacity % 16 == 0 and tokens % 16 == 0 and width % 512 == 0:
        next_input, previous_grad = fused(
            forward_input[0], forward_route[0], forward_weight[0],
            backward_input[0], backward_route[0], backward_weight[0],
            output_grad[0], norm_gain, gate_weight[0], up_weight[0], down_weight[0],
            experts, group, capacity,
        )
        return (next_input[None], previous_grad[None])
    mine = lax.axis_index("expert") // group
    gain = norm_gain[0]
    own = (gate_weight[0], up_weight[0], down_weight[0])
    other = tuple(swapped(w, 2) for w in own)
    weights = (own, other)

    ahead_wide, ahead_scale, ahead_normed = normalize(forward_input[0], gain)
    behind_wide, behind_scale, behind_normed = normalize(backward_input[0], gain)
    cotangent = output_grad[0].astype(jnp.float32)
    routed_grad = (
        jnp.repeat(cotangent, top, axis=0) * backward_weight[0].reshape(-1)[:, None]
    ).astype(jnp.bfloat16)
    ahead_slots = slot_matrix(forward_route[0], experts, capacity, mine)
    behind_slots = slot_matrix(backward_route[0], experts, capacity, mine)

    def gathered(matrix, rows):
        pieces = across(to_slots(matrix, rows), experts, group, 1)
        near = jnp.concatenate(pieces, axis=0)
        far = jnp.concatenate(
            [swapped(pieces[0], 1), swapped(jnp.concatenate(pieces[1:], axis=0), 1)], axis=0
        )
        return near, far

    def returned(near_sum, far_sum):
        total = (near_sum + swapped(far_sum.astype(jnp.bfloat16), 1)).astype(jnp.bfloat16)
        return jnp.concatenate(across(total, experts, group, -1), axis=0)

    ahead_near, ahead_far = gathered(ahead_slots, jnp.repeat(ahead_normed, top, axis=0))
    behind_near, behind_far = gathered(behind_slots, jnp.repeat(behind_normed, top, axis=0))
    grad_near, grad_far = gathered(behind_slots, routed_grad)

    ahead_back = returned(forward_sum(ahead_near, weights), forward_sum(ahead_far, weights))
    ahead_values = from_slots(ahead_slots, ahead_back)
    mixed = jnp.sum(
        ahead_values.reshape(tokens, top, width) * forward_weight[0][:, :, None], axis=1
    )
    section_out = (ahead_wide + mixed).astype(jnp.bfloat16)
    next_input = passed_along(section_out, "pipe", 1)

    behind_back = returned(
        backward_sum(behind_near, grad_near, weights), backward_sum(behind_far, grad_far, weights)
    )
    behind_values = from_slots(behind_slots, behind_back)
    normed_grad = jnp.sum(behind_values.reshape(tokens, top, width), axis=1)
    unit = behind_wide * behind_scale
    unit_grad = gain * normed_grad
    section_grad = cotangent + behind_scale * (
        unit_grad - unit * jnp.mean(unit_grad * unit, axis=-1, keepdims=True)
    )
    section_grad = section_grad.astype(jnp.bfloat16)
    previous_grad = passed_along(section_grad, "pipe", -1)
    return (next_input[None], previous_grad[None])


def solution(mesh):
    return jax.shard_map(
        per_device,
        mesh=mesh,
        in_specs=(
            P("pipe", "expert", None),
            P("pipe", "expert", None),
            P("pipe", "expert", None),
            P("pipe", "expert", None),
            P("pipe", "expert", None),
            P("pipe", "expert", None),
            P("pipe", "expert", None),
            P("pipe", None),
            P("pipe", None, "expert"),
            P("pipe", None, "expert"),
            P("pipe", "expert", None),
        ),
        out_specs=(P("pipe", "expert", None), P("pipe", "expert", None)),
        check_vma=False,
    )
```

```python
import functools

import jax
import jax.numpy as jnp
from jax import lax
from jax.experimental import pallas as pl
from jax.experimental.pallas import tpu as pltpu
from jax.sharding import PartitionSpec as P

HID = 1024


EPS = 1e-06


def passed_along(array, axis, by):
    devices = lax.axis_size(axis)
    return lax.ppermute(array, axis, [(i, (i + by) % devices) for i in range(devices)])


def swapped(array, bit):
    devices = lax.axis_size("expert")
    return lax.ppermute(array, "expert", [(i, i ^ bit) for i in range(devices)])


def normalize(values, gain):
    widened = values.astype(jnp.float32)
    scale = lax.rsqrt(jnp.mean(widened * widened, axis=-1, keepdims=True) + EPS)
    return (widened, scale, (widened * scale * gain).astype(jnp.bfloat16))


def slot_matrix(routes, experts, capacity, mine):
    flat = lax.rem(routes.reshape(-1) + (experts - mine), experts)
    pairs = flat.shape[0]
    onehot = flat[:, None] == jnp.arange(experts, dtype=jnp.int32)[None, :]
    before = jnp.arange(pairs)[:, None] > jnp.arange(pairs)[None, :]
    counts = jnp.dot(
        before.astype(jnp.bfloat16), onehot.astype(jnp.bfloat16), preferred_element_type=jnp.float32
    )
    ranks = jnp.sum(jnp.where(onehot, counts, 0.0), axis=1).astype(jnp.int32)
    target = flat * capacity + ranks
    slots = jnp.arange(experts * capacity, dtype=jnp.int32)
    return (slots[:, None] == target[None, :]).astype(jnp.bfloat16)


def to_slots(matrix, rows):
    return jnp.dot(matrix, rows, preferred_element_type=jnp.float32).astype(jnp.bfloat16)


def from_slots(matrix, rows):
    return lax.dot_general(
        matrix, rows, (((0,), (0,)), ((), ())), preferred_element_type=jnp.float32
    )


def across(slots, experts, group, sign):
    blocks = jnp.split(slots, experts, axis=0)
    return blocks[:1] + [
        passed_along(blocks[k], "expert", sign * group * k) for k in range(1, experts)
    ]


def dot(a, b):
    return jnp.dot(a, b, preferred_element_type=jnp.float32)


def dot_t(a, b):
    return lax.dot_general(a, b, (((1,), (1,)), ((), ())), preferred_element_type=jnp.float32)


def forward_sum(rows, weights):
    total = None
    for gate, up, down in weights:
        hidden = (jax.nn.silu(dot(rows, gate)) * dot(rows, up)).astype(jnp.bfloat16)
        part = dot(hidden, down)
        total = part if total is None else total + part
    return total


def backward_sum(rows, grads, weights):
    total = None
    for gate, up, down in weights:
        gate_back = dot(rows, gate)
        up_back = dot(rows, up)
        hidden_grad = dot_t(grads, down)
        sig = jax.nn.sigmoid(gate_back)
        gate_grad = (hidden_grad * up_back * sig * (1.0 + gate_back * (1.0 - sig))).astype(
            jnp.bfloat16
        )
        up_grad = (hidden_grad * gate_back * sig).astype(jnp.bfloat16)
        part = dot_t(gate_grad, gate) + dot_t(up_grad, up)
        total = part if total is None else total + part
    return total


MESH = pl.DeviceIdType.MESH
BF = jnp.bfloat16
F32 = jnp.float32


def slot_masks(col, row, experts, cap, mine):
    def relative(route):
        return jnp.where(route >= mine, route - mine, route - mine + experts).astype(F32)

    tokens, rows = col.shape[0], experts * cap
    rel_c, rel_r = relative(col), relative(row)
    first = lax.broadcasted_iota(jnp.int32, (tokens, tokens), 0)
    second = lax.broadcasted_iota(jnp.int32, (tokens, tokens), 1)
    same = jnp.where(rel_c == rel_r, 1.0, 0.0)
    rank_c = jnp.sum(jnp.where(first > second, same, 0.0), axis=1, keepdims=True)
    rank_r = jnp.sum(jnp.where(first < second, same, 0.0), axis=0, keepdims=True)
    down = lax.broadcasted_iota(jnp.int32, (rows, tokens), 0).astype(F32)
    along = lax.broadcasted_iota(jnp.int32, (tokens, rows), 1).astype(F32)
    to_slot = jnp.where(down == rel_r * cap + rank_r, 1.0, 0.0).astype(BF)
    from_slot = jnp.where(along == rel_c * cap + rank_c, 1.0, 0.0).astype(BF)
    return to_slot, from_slot


def section_kernel(
    cfg,
    fx, bx, og, gain, fw, bw, fr_c, fr_r, br_c, br_r, gate, up, down,
    next_ref, prev_ref,
    g0, u0, g1, u1, dd, rows_f, rows_b, rows_g, out_f, out_b, out_g,
    acc_a, acc_b, acc_c, hid, ggr, ugr, far_f, far_b, x_f, x_b, back_f, back_b,
    ret_f, ret_b, ngr, fin_f, fin_b, tmp, scale_b, s_f, s_b, st_f, st_b,
    w_sem, d_s, d_r, wl_sem, in_s, in_r, xl_s, xl_r, xf_s, xf_r, xo_s, xo_r, re_s, re_r, pi_s, pi_r,
):
    experts, group, cap, chunks, cw = cfg
    tokens, width = fx.shape
    rows = experts * cap
    hd = gate.shape[1]
    n = experts * group
    me = lax.axis_index("expert")
    pipe = lax.axis_index("pipe")
    pipes = lax.axis_size("pipe")
    xp = me + 1 - 2 * lax.rem(me, 2)
    zp = me + 2 - 4 * lax.rem(lax.div(me, 2), 2)
    onward = {"pipe": lax.rem(pipe + 1, pipes)}
    behind = {"pipe": lax.rem(pipe + pipes - 1, pipes)}

    def ahead_of(k):
        return {"expert": lax.rem(me + group * k, n)}

    def back_of(k):
        return {"expert": lax.rem(me + n - group * k, n)}

    def remote(src, dst, ss, rs, dev):
        return pltpu.make_async_remote_copy(
            src_ref=src, dst_ref=dst, send_sem=ss, recv_sem=rs, device_id=dev, device_id_type=MESH
        )

    barrier = pltpu.get_barrier_semaphore()
    peers = [ahead_of(k) for k in range(1, experts)]
    peers += [{"expert": xp}, {"expert": zp}, onward, behind]
    for peer in peers:
        pl.semaphore_signal(barrier, inc=1, device_id=peer, device_id_type=MESH)
    pl.semaphore_wait(barrier, len(peers))

    heavy = [
        remote(src, dst, w_sem.at[0, i], w_sem.at[1, i], {"expert": zp})
        for i, (src, dst) in enumerate(((gate, g1), (up, u1)))
    ]
    for copy in heavy:
        copy.start()
    local = [
        pltpu.make_async_copy(src, dst, wl_sem.at[i])
        for i, (src, dst) in enumerate(((gate, g0), (up, u0), (down, dd.at[pl.ds(0, hd)])))
    ]

    for copy in local:
        copy.start()

    def col(c):
        return pl.ds(pl.multiple_of(c * cw, cw), cw)

    def each_chunk(body):
        def step(c, carry):
            body(c)
            return carry

        lax.fori_loop(0, chunks, step, 0)

    def down_chunk(c):
        return remote(
            down.at[:, col(c)], dd.at[pl.ds(hd, hd), col(c)], d_s.at[c], d_r.at[c], {"expert": zp}
        )

    def each_band(body):
        def step(i, carry):
            body(pl.ds(pl.multiple_of(i * 16, 16), 16))
            return carry

        lax.fori_loop(0, tokens // 16, step, 0)

    def norm_into(src, keep):
        def body(band):
            wide = src[band, :].astype(F32)
            scale = lax.rsqrt(jnp.mean(wide * wide, axis=-1, keepdims=True) + EPS)
            tmp[band, :] = (wide * scale * gain[...]).astype(BF)
            if keep is not None:
                keep[band, :] = scale

        each_band(body)

    def weigh_into():
        def body(band):
            tmp[band, :] = (og[band, :].astype(F32) * bw[band, :]).astype(BF)

        each_band(body)

    def crossing(a, out, into):
        return [
            remote(
                out.at[pl.ds((k - 1) * cap, cap)],
                into.at[pl.ds(k * cap, cap)],
                in_s.at[a, k - 1],
                in_r.at[a, k - 1],
                ahead_of(k),
            )
            for k in range(1, experts)
        ]

    def near_x(a, into):
        return remote(
            into.at[pl.ds(0, cap)], into.at[pl.ds(rows, cap)], xl_s.at[a], xl_r.at[a], {"expert": xp}
        )

    def far_x(a, into):
        return remote(
            into.at[pl.ds(cap, rows - cap)],
            into.at[pl.ds(rows + cap, rows - cap)],
            xf_s.at[a],
            xf_r.at[a],
            {"expert": xp},
        )

    def place(matrix, out, into):
        def body(c):
            picked = dot(matrix[...], tmp[:, col(c)]).astype(BF)
            into[pl.ds(0, cap), col(c)] = picked[:cap]
            out[:, col(c)] = picked[cap:]

        each_chunk(body)

    mine = lax.div(me, group)
    s_f[...], st_f[...] = slot_masks(fr_c[...], fr_r[...], experts, cap, mine)
    s_b[...], st_b[...] = slot_masks(br_c[...], br_r[...], experts, cap, mine)
    sets = ((s_f, out_f, rows_f), (s_b, out_b, rows_b), (s_b, out_g, rows_g))
    pending = []
    crossings, nears, fars = [], [], []
    for a, (matrix, out, into) in enumerate(sets):
        if a == 0:
            norm_into(fx, None)
        elif a == 1:
            norm_into(bx, scale_b)
        else:
            weigh_into()
        place(matrix, out, into)
        cross = crossing(a, out, into)
        for copy in cross:
            copy.start()
        near = near_x(a, into)
        near.start()
        crossings.append(cross)
        nears.append(near)
        pending += cross + [near]

    for a in range(3):
        for copy in crossings[a]:
            copy.wait_recv()
        far = far_x(a, sets[a][2])
        far.start()
        fars.append(far)
        pending.append(far)
    for copy in heavy:
        copy.wait_send()

    def start_down(c):
        down_chunk(c).start()

    each_chunk(start_down)
    for copy in local:
        copy.wait()

    def first(source, weight, acc):
        acc[...] = jnp.zeros_like(acc)

        def body(c):
            acc[...] += dot(source[:, col(c)], weight[col(c), :])

        each_chunk(body)

    def add_t(half, c):
        acc_c[...] += dot_t(rows_g[:, col(c)], dd[pl.ds(half * hd, hd), col(c)])

    def hidden_half(half, gw, uw):
        first(rows_f, gw, acc_a)
        first(rows_f, uw, acc_b)
        pre = acc_a[...]
        hid[:, pl.ds(half * hd, hd)] = (pre * jax.nn.sigmoid(pre) * acc_b[...]).astype(BF)

    def grads_start(gw, uw):
        first(rows_b, gw, acc_a)
        first(rows_b, uw, acc_b)
        acc_c[...] = jnp.zeros_like(acc_c)

    def grads_end(half):
        pre, upb, hg = acc_a[...], acc_b[...], acc_c[...]
        sig = jax.nn.sigmoid(pre)
        ggr[:, pl.ds(half * hd, hd)] = (hg * upb * sig * (1.0 + pre * (1.0 - sig))).astype(BF)
        ugr[:, pl.ds(half * hd, hd)] = (hg * pre * sig).astype(BF)

    nears[0].wait_recv()
    fars[0].wait_recv()
    hidden_half(0, g0, u0)
    for a in (1, 2):
        nears[a].wait_recv()
        fars[a].wait_recv()
    grads_start(g0, u0)
    each_chunk(functools.partial(add_t, 0))
    grads_end(0)
    for copy in heavy:
        copy.wait_recv()
    hidden_half(1, g1, u1)
    grads_start(g1, u1)

    def sum_f(at, c):
        return dot(hid[pl.ds(at, rows), :], dd[:, col(c)])

    def sum_b(at, c):
        ga, ua = ggr[pl.ds(at, rows), :], ugr[pl.ds(at, rows), :]
        total = dot_t(ga[:, :hd], g0[col(c), :]) + dot_t(ga[:, hd:], g1[col(c), :])
        return total + dot_t(ua[:, :hd], u0[col(c), :]) + dot_t(ua[:, hd:], u1[col(c), :])

    def x_out(a, c):
        src, dst = ((far_f, x_f), (far_b, x_b))[a]
        return remote(src.at[c], dst.at[c], xo_s.at[a, c], xo_r.at[a, c], {"expert": xp})

    def going_back(a, c):
        src, dst = ((ret_f, back_f), (ret_b, back_b))[a]
        return [
            remote(
                src.at[c, pl.ds((k - 1) * cap, cap)],
                dst.at[c, pl.ds(k * cap, cap)],
                re_s.at[a, c, k - 1],
                re_r.at[a, c, k - 1],
                back_of(k),
            )
            for k in range(1, experts)
        ]

    def leaving(a, c):
        src, dst, dev = ((fin_f, next_ref, onward), (fin_b, prev_ref, behind))[a]
        return remote(src.at[c], dst.at[:, col(c)], pi_s.at[a, c], pi_r.at[a, c], dev)

    def far_step_f(c):
        down_chunk(c).wait_recv()
        far_f[c] = sum_f(rows, c).astype(BF)
        x_out(0, c).start()
        add_t(1, c)

    each_chunk(far_step_f)
    grads_end(1)

    def far_step_b(c):
        far_b[c] = sum_b(rows, c).astype(BF)
        x_out(1, c).start()

    each_chunk(far_step_b)

    def near_step(a, summed, x_in, back, ret):
        def body(c):
            total = summed(0, c)
            x_out(a, c).wait_recv()
            total = (total + x_in[c].astype(F32)).astype(BF)
            back[c, pl.ds(0, cap), :] = total[:cap]
            ret[c] = total[cap:]
            for copy in going_back(a, c):
                copy.start()

        return body

    each_chunk(near_step(0, sum_f, x_f, back_f, ret_f))
    near_b = near_step(1, sum_b, x_b, back_b, ret_b)

    def final_f(c):
        for copy in going_back(0, c):
            copy.wait_recv()
        values = dot(st_f[...], back_f[c])
        fin_f[c] = (fx[:, col(c)].astype(F32) + fw[...] * values).astype(BF)
        leaving(0, c).start()

    def near_b_final_f(c):
        near_b(c)
        final_f(c)

    each_chunk(near_b_final_f)

    def gather_b(c, carry):
        for copy in going_back(1, c):
            copy.wait_recv()
        unit_grad = gain[:, col(c)] * dot(st_b[...], back_b[c])
        ngr[c] = unit_grad
        unit = bx[:, col(c)].astype(F32) * scale_b[...]
        return carry + jnp.sum(unit_grad * unit, axis=-1, keepdims=True)

    mean = lax.fori_loop(0, chunks, gather_b, jnp.zeros((tokens, 1), F32)) / width

    def final_b(c):
        unit = bx[:, col(c)].astype(F32) * scale_b[...]
        grad = og[:, col(c)].astype(F32) + scale_b[...] * (ngr[c] - unit * mean)
        fin_b[c] = grad.astype(BF)
        leaving(1, c).start()

    each_chunk(final_b)

    for copy in pending:
        copy.wait_send()

    def drain(c):
        down_chunk(c).wait_send()
        for a in range(2):
            x_out(a, c).wait_send()
            for copy in going_back(a, c):
                copy.wait_send()
            leaving(a, c).wait()

    each_chunk(drain)


def fused(fi, fr, fwt, bi, br, bwt, og, gain, gate, up, down, experts, group, cap):
    tokens, width = fi.shape
    hd = gate.shape[1]
    rows = experts * cap
    cw = 512
    chunks = width // cw
    vm = pltpu.VMEM
    sem = pltpu.SemaphoreType.DMA
    others = experts - 1
    scratch = [vm((width, hd), BF)] * 4 + [vm((2 * hd, width), BF)]
    scratch += [vm((2 * rows, width), BF)] * 3 + [vm((others * cap, width), BF)] * 3
    scratch += [vm((2 * rows, hd), F32)] * 3 + [vm((2 * rows, 2 * hd), BF)] * 3
    scratch += [vm((chunks, rows, cw), BF)] * 6 + [vm((chunks, others * cap, cw), BF)] * 2
    scratch += [vm((chunks, tokens, cw), F32)] + [vm((chunks, tokens, cw), BF)] * 2
    scratch += [vm((tokens, width), BF), vm((tokens, 1), F32)]
    scratch += [vm((rows, tokens), BF)] * 2 + [vm((tokens, rows), BF)] * 2
    scratch += [sem((2, 2)), sem((chunks,)), sem((chunks,)), sem((3,)), sem((3, others)), sem((3, others))]
    scratch += [sem((3,))] * 4 + [sem((2, chunks))] * 2
    scratch += [sem((2, chunks, others))] * 2 + [sem((2, chunks))] * 2
    out = jax.ShapeDtypeStruct((tokens, width), BF)
    anywhere = pl.BlockSpec(memory_space=pl.ANY)
    return pl.pallas_call(
        functools.partial(section_kernel, (experts, group, cap, chunks, cw)),
        out_shape=(out, out),
        in_specs=[pl.BlockSpec(memory_space=vm)] * 10 + [anywhere] * 3,
        out_specs=(anywhere, anywhere),
        scratch_shapes=scratch,
        compiler_params=pltpu.CompilerParams(
            collective_id=0, has_side_effects=True, vmem_limit_bytes=58 * 1024 * 1024
        ),
    )(fi, bi, og, gain, fwt, bwt, fr, fr.T, br, br.T, gate, up, down)


def per_device(
    forward_input,
    forward_route,
    forward_weight,
    backward_input,
    backward_route,
    backward_weight,
    output_grad,
    norm_gain,
    gate_weight,
    up_weight,
    down_weight,
):
    group = HID // gate_weight.shape[2]
    assert group == 4
    experts = lax.axis_size("expert") // group
    tokens = forward_input.shape[1]
    top = forward_route.shape[2]
    width = forward_input.shape[2]
    capacity = max(2, 3 * tokens * top // (2 * experts))
    if top == 1 and capacity % 16 == 0 and tokens % 16 == 0 and width % 512 == 0:
        next_input, previous_grad = fused(
            forward_input[0], forward_route[0], forward_weight[0],
            backward_input[0], backward_route[0], backward_weight[0],
            output_grad[0], norm_gain, gate_weight[0], up_weight[0], down_weight[0],
            experts, group, capacity,
        )
        return (next_input[None], previous_grad[None])
    mine = lax.axis_index("expert") // group
    gain = norm_gain[0]
    own = (gate_weight[0], up_weight[0], down_weight[0])
    other = tuple(swapped(w, 2) for w in own)
    weights = (own, other)

    ahead_wide, ahead_scale, ahead_normed = normalize(forward_input[0], gain)
    behind_wide, behind_scale, behind_normed = normalize(backward_input[0], gain)
    cotangent = output_grad[0].astype(jnp.float32)
    routed_grad = (
        jnp.repeat(cotangent, top, axis=0) * backward_weight[0].reshape(-1)[:, None]
    ).astype(jnp.bfloat16)
    ahead_slots = slot_matrix(forward_route[0], experts, capacity, mine)
    behind_slots = slot_matrix(backward_route[0], experts, capacity, mine)

    def gathered(matrix, rows):
        pieces = across(to_slots(matrix, rows), experts, group, 1)
        near = jnp.concatenate(pieces, axis=0)
        far = jnp.concatenate(
            [swapped(pieces[0], 1), swapped(jnp.concatenate(pieces[1:], axis=0), 1)], axis=0
        )
        return near, far

    def returned(near_sum, far_sum):
        total = (near_sum + swapped(far_sum.astype(jnp.bfloat16), 1)).astype(jnp.bfloat16)
        return jnp.concatenate(across(total, experts, group, -1), axis=0)

    ahead_near, ahead_far = gathered(ahead_slots, jnp.repeat(ahead_normed, top, axis=0))
    behind_near, behind_far = gathered(behind_slots, jnp.repeat(behind_normed, top, axis=0))
    grad_near, grad_far = gathered(behind_slots, routed_grad)

    ahead_back = returned(forward_sum(ahead_near, weights), forward_sum(ahead_far, weights))
    ahead_values = from_slots(ahead_slots, ahead_back)
    mixed = jnp.sum(
        ahead_values.reshape(tokens, top, width) * forward_weight[0][:, :, None], axis=1
    )
    section_out = (ahead_wide + mixed).astype(jnp.bfloat16)
    next_input = passed_along(section_out, "pipe", 1)

    behind_back = returned(
        backward_sum(behind_near, grad_near, weights), backward_sum(behind_far, grad_far, weights)
    )
    behind_values = from_slots(behind_slots, behind_back)
    normed_grad = jnp.sum(behind_values.reshape(tokens, top, width), axis=1)
    unit = behind_wide * behind_scale
    unit_grad = gain * normed_grad
    section_grad = cotangent + behind_scale * (
        unit_grad - unit * jnp.mean(unit_grad * unit, axis=-1, keepdims=True)
    )
    section_grad = section_grad.astype(jnp.bfloat16)
    previous_grad = passed_along(section_grad, "pipe", -1)
    return (next_input[None], previous_grad[None])


def solution(mesh):
    return jax.shard_map(
        per_device,
        mesh=mesh,
        in_specs=(
            P("pipe", "expert", None),
            P("pipe", "expert", None),
            P("pipe", "expert", None),
            P("pipe", "expert", None),
            P("pipe", "expert", None),
            P("pipe", "expert", None),
            P("pipe", "expert", None),
            P("pipe", None),
            P("pipe", None, "expert"),
            P("pipe", None, "expert"),
            P("pipe", "expert", None),
        ),
        out_specs=(P("pipe", "expert", None), P("pipe", "expert", None)),
        check_vma=False,
    )
```

```python
import functools

import jax
import jax.numpy as jnp
from jax import lax
from jax.experimental import pallas as pl
from jax.experimental.pallas import tpu as pltpu
from jax.sharding import PartitionSpec as P

HID = 1024


EPS = 1e-06


def passed_along(array, axis, by):
    devices = lax.axis_size(axis)
    return lax.ppermute(array, axis, [(i, (i + by) % devices) for i in range(devices)])


def swapped(array, bit):
    devices = lax.axis_size("expert")
    return lax.ppermute(array, "expert", [(i, i ^ bit) for i in range(devices)])


def normalize(values, gain):
    widened = values.astype(jnp.float32)
    scale = lax.rsqrt(jnp.mean(widened * widened, axis=-1, keepdims=True) + EPS)
    return (widened, scale, (widened * scale * gain).astype(jnp.bfloat16))


def slot_matrix(routes, experts, capacity, mine):
    flat = lax.rem(routes.reshape(-1) + (experts - mine), experts)
    pairs = flat.shape[0]
    onehot = flat[:, None] == jnp.arange(experts, dtype=jnp.int32)[None, :]
    before = jnp.arange(pairs)[:, None] > jnp.arange(pairs)[None, :]
    counts = jnp.dot(
        before.astype(jnp.bfloat16), onehot.astype(jnp.bfloat16), preferred_element_type=jnp.float32
    )
    ranks = jnp.sum(jnp.where(onehot, counts, 0.0), axis=1).astype(jnp.int32)
    target = flat * capacity + ranks
    slots = jnp.arange(experts * capacity, dtype=jnp.int32)
    return (slots[:, None] == target[None, :]).astype(jnp.bfloat16)


def to_slots(matrix, rows):
    return jnp.dot(matrix, rows, preferred_element_type=jnp.float32).astype(jnp.bfloat16)


def from_slots(matrix, rows):
    return lax.dot_general(
        matrix, rows, (((0,), (0,)), ((), ())), preferred_element_type=jnp.float32
    )


def across(slots, experts, group, sign):
    blocks = jnp.split(slots, experts, axis=0)
    return blocks[:1] + [
        passed_along(blocks[k], "expert", sign * group * k) for k in range(1, experts)
    ]


def dot(a, b):
    return jnp.dot(a, b, preferred_element_type=jnp.float32)


def dot_t(a, b):
    return lax.dot_general(a, b, (((1,), (1,)), ((), ())), preferred_element_type=jnp.float32)


def forward_sum(rows, weights):
    total = None
    for gate, up, down in weights:
        hidden = (jax.nn.silu(dot(rows, gate)) * dot(rows, up)).astype(jnp.bfloat16)
        part = dot(hidden, down)
        total = part if total is None else total + part
    return total


def backward_sum(rows, grads, weights):
    total = None
    for gate, up, down in weights:
        gate_back = dot(rows, gate)
        up_back = dot(rows, up)
        hidden_grad = dot_t(grads, down)
        sig = jax.nn.sigmoid(gate_back)
        gate_grad = (hidden_grad * up_back * sig * (1.0 + gate_back * (1.0 - sig))).astype(
            jnp.bfloat16
        )
        up_grad = (hidden_grad * gate_back * sig).astype(jnp.bfloat16)
        part = dot_t(gate_grad, gate) + dot_t(up_grad, up)
        total = part if total is None else total + part
    return total


MESH = pl.DeviceIdType.MESH
BF = jnp.bfloat16
F32 = jnp.float32


def slot_masks(col, row, experts, cap, mine):
    def relative(route):
        return jnp.where(route >= mine, route - mine, route - mine + experts).astype(F32)

    tokens, rows = col.shape[0], experts * cap
    rel_c, rel_r = relative(col), relative(row)
    first = lax.broadcasted_iota(jnp.int32, (tokens, tokens), 0)
    second = lax.broadcasted_iota(jnp.int32, (tokens, tokens), 1)
    same = jnp.where(rel_c == rel_r, 1.0, 0.0)
    rank_c = jnp.sum(jnp.where(first > second, same, 0.0), axis=1, keepdims=True)
    rank_r = jnp.sum(jnp.where(first < second, same, 0.0), axis=0, keepdims=True)
    down = lax.broadcasted_iota(jnp.int32, (rows, tokens), 0).astype(F32)
    along = lax.broadcasted_iota(jnp.int32, (tokens, rows), 1).astype(F32)
    to_slot = jnp.where(down == rel_r * cap + rank_r, 1.0, 0.0).astype(BF)
    from_slot = jnp.where(along == rel_c * cap + rank_c, 1.0, 0.0).astype(BF)
    return to_slot, from_slot


def section_kernel(
    cfg,
    fx, bx, og, gain, fw, bw, fr_c, fr_r, br_c, br_r, gate, up, down,
    next_ref, prev_ref,
    g0, u0, g1, u1, dd, rows_f, rows_b, rows_g, out_f, out_b, out_g,
    acc_a, acc_b, acc_c, hid, ggr, ugr, far_f, far_b, x_f, x_b, back_f, back_b,
    ret_f, ret_b, ngr, fin_f, fin_b, tmp, scale_b, s_f, s_b, st_f, st_b, sum_f, sum_b,
    w_sem, d_s, d_r, wl_sem, in_s, in_r, xl_s, xl_r, xf_s, xf_r, xo_s, xo_r, re_s, re_r, pi_s, pi_r,
):
    experts, group, cap, chunks, cw = cfg
    tokens, width = fx.shape
    rows = experts * cap
    hd = gate.shape[1]
    n = experts * group
    me = lax.axis_index("expert")
    pipe = lax.axis_index("pipe")
    pipes = lax.axis_size("pipe")
    xp = me + 1 - 2 * lax.rem(me, 2)
    zp = me + 2 - 4 * lax.rem(lax.div(me, 2), 2)
    onward = {"pipe": lax.rem(pipe + 1, pipes)}
    behind = {"pipe": lax.rem(pipe + pipes - 1, pipes)}

    def ahead_of(k):
        return {"expert": lax.rem(me + group * k, n)}

    def back_of(k):
        return {"expert": lax.rem(me + n - group * k, n)}

    def remote(src, dst, ss, rs, dev):
        return pltpu.make_async_remote_copy(
            src_ref=src, dst_ref=dst, send_sem=ss, recv_sem=rs, device_id=dev, device_id_type=MESH
        )

    barrier = pltpu.get_barrier_semaphore()
    peers = [ahead_of(k) for k in range(1, experts)]
    peers += [{"expert": xp}, {"expert": zp}, onward, behind]
    for peer in peers:
        pl.semaphore_signal(barrier, inc=1, device_id=peer, device_id_type=MESH)
    pl.semaphore_wait(barrier, len(peers))

    heavy = [
        remote(src, dst, w_sem.at[0, i], w_sem.at[1, i], {"expert": zp})
        for i, (src, dst) in enumerate(((gate, g1), (up, u1)))
    ]
    for copy in heavy:
        copy.start()
    local = [
        pltpu.make_async_copy(src, dst, wl_sem.at[i])
        for i, (src, dst) in enumerate(((gate, g0), (up, u0), (down, dd.at[pl.ds(0, hd)])))
    ]

    for copy in local:
        copy.start()

    def col(c):
        return pl.ds(pl.multiple_of(c * cw, cw), cw)

    def each_chunk(body):
        def step(c, carry):
            body(c)
            return carry

        lax.fori_loop(0, chunks, step, 0)

    def down_chunk(c):
        return remote(
            down.at[:, col(c)], dd.at[pl.ds(hd, hd), col(c)], d_s.at[c], d_r.at[c], {"expert": zp}
        )

    def each_band(body):
        def step(i, carry):
            body(pl.ds(pl.multiple_of(i * 16, 16), 16))
            return carry

        lax.fori_loop(0, tokens // 16, step, 0)

    def norm_into(src, keep):
        def body(band):
            wide = src[band, :].astype(F32)
            scale = lax.rsqrt(jnp.mean(wide * wide, axis=-1, keepdims=True) + EPS)
            tmp[band, :] = (wide * scale * gain[...]).astype(BF)
            if keep is not None:
                keep[band, :] = scale

        each_band(body)

    def weigh_into():
        def body(band):
            tmp[band, :] = (og[band, :].astype(F32) * bw[band, :]).astype(BF)

        each_band(body)

    def crossing(a, out, into):
        return [
            remote(
                out.at[pl.ds((k - 1) * cap, cap)],
                into.at[pl.ds(k * cap, cap)],
                in_s.at[a, k - 1],
                in_r.at[a, k - 1],
                ahead_of(k),
            )
            for k in range(1, experts)
        ]

    def near_x(a, into):
        return remote(
            into.at[pl.ds(0, cap)], into.at[pl.ds(rows, cap)], xl_s.at[a], xl_r.at[a], {"expert": xp}
        )

    def far_x(a, into):
        return remote(
            into.at[pl.ds(cap, rows - cap)],
            into.at[pl.ds(rows + cap, rows - cap)],
            xf_s.at[a],
            xf_r.at[a],
            {"expert": xp},
        )

    def place(matrix, out, into):
        def body(c):
            picked = dot(matrix[...], tmp[:, col(c)]).astype(BF)
            into[pl.ds(0, cap), col(c)] = picked[:cap]
            out[:, col(c)] = picked[cap:]

        each_chunk(body)

    mine = lax.div(me, group)
    s_f[...], st_f[...] = slot_masks(fr_c[...], fr_r[...], experts, cap, mine)
    s_b[...], st_b[...] = slot_masks(br_c[...], br_r[...], experts, cap, mine)
    sets = ((s_f, out_f, rows_f), (s_b, out_b, rows_b), (s_b, out_g, rows_g))
    pending = []
    crossings, nears, fars = [], [], []
    for a, (matrix, out, into) in enumerate(sets):
        if a == 0:
            norm_into(fx, None)
        elif a == 1:
            norm_into(bx, scale_b)
        else:
            weigh_into()
        place(matrix, out, into)
        cross = crossing(a, out, into)
        for copy in cross:
            copy.start()
        near = near_x(a, into)
        near.start()
        crossings.append(cross)
        nears.append(near)
        pending += cross + [near]

    for a in range(3):
        for copy in crossings[a]:
            copy.wait_recv()
        far = far_x(a, sets[a][2])
        far.start()
        fars.append(far)
        pending.append(far)
    for copy in heavy:
        copy.wait_send()

    def start_down(c):
        down_chunk(c).start()

    each_chunk(start_down)
    for copy in local:
        copy.wait()

    def first(source, weight, acc):
        acc[...] = jnp.zeros_like(acc)

        def body(c):
            acc[...] += dot(source[:, col(c)], weight[col(c), :])

        each_chunk(body)

    def add_t(half, c):
        acc_c[...] += dot_t(rows_g[:, col(c)], dd[pl.ds(half * hd, hd), col(c)])

    def hidden_half(half, gw, uw):
        first(rows_f, gw, acc_a)
        first(rows_f, uw, acc_b)
        pre = acc_a[...]
        hid[:, pl.ds(half * hd, hd)] = (pre * jax.nn.sigmoid(pre) * acc_b[...]).astype(BF)

    def grads_start(gw, uw):
        first(rows_b, gw, acc_a)
        first(rows_b, uw, acc_b)
        acc_c[...] = jnp.zeros_like(acc_c)

    def grads_end(half):
        pre, upb, hg = acc_a[...], acc_b[...], acc_c[...]
        sig = jax.nn.sigmoid(pre)
        ggr[:, pl.ds(half * hd, hd)] = (hg * upb * sig * (1.0 + pre * (1.0 - sig))).astype(BF)
        ugr[:, pl.ds(half * hd, hd)] = (hg * pre * sig).astype(BF)

    nears[0].wait_recv()
    fars[0].wait_recv()
    hidden_half(0, g0, u0)

    def own_f(c):
        sum_f[c] = dot(hid[:, pl.ds(0, hd)], dd[pl.ds(0, hd), col(c)])

    each_chunk(own_f)
    for a in (1, 2):
        nears[a].wait_recv()
        fars[a].wait_recv()
    grads_start(g0, u0)
    each_chunk(functools.partial(add_t, 0))
    grads_end(0)

    def own_b(c):
        part = dot_t(ggr[:, pl.ds(0, hd)], g0[col(c), :])
        sum_b[c] = part + dot_t(ugr[:, pl.ds(0, hd)], u0[col(c), :])

    each_chunk(own_b)
    for copy in heavy:
        copy.wait_recv()
    hidden_half(1, g1, u1)
    grads_start(g1, u1)

    def x_out(a, c):
        src, dst = ((far_f, x_f), (far_b, x_b))[a]
        return remote(src.at[c], dst.at[c], xo_s.at[a, c], xo_r.at[a, c], {"expert": xp})

    def going_back(a, c):
        src, dst = ((ret_f, back_f), (ret_b, back_b))[a]
        return [
            remote(
                src.at[c, pl.ds((k - 1) * cap, cap)],
                dst.at[c, pl.ds(k * cap, cap)],
                re_s.at[a, c, k - 1],
                re_r.at[a, c, k - 1],
                back_of(k),
            )
            for k in range(1, experts)
        ]

    def leaving(a, c):
        src, dst, dev = ((fin_f, next_ref, onward), (fin_b, prev_ref, behind))[a]
        return remote(src.at[c], dst.at[:, col(c)], pi_s.at[a, c], pi_r.at[a, c], dev)

    def far_step_f(c):
        down_chunk(c).wait_recv()
        total = sum_f[c] + dot(hid[:, pl.ds(hd, hd)], dd[pl.ds(hd, hd), col(c)])
        far_f[c] = total[rows:].astype(BF)
        x_out(0, c).start()
        sum_f[c, pl.ds(0, rows), :] = total[:rows]
        add_t(1, c)

    each_chunk(far_step_f)
    grads_end(1)

    def far_step_b(c):
        total = sum_b[c] + dot_t(ggr[:, pl.ds(hd, hd)], g1[col(c), :])
        total = total + dot_t(ugr[:, pl.ds(hd, hd)], u1[col(c), :])
        far_b[c] = total[rows:].astype(BF)
        x_out(1, c).start()
        sum_b[c, pl.ds(0, rows), :] = total[:rows]

    each_chunk(far_step_b)

    def near_step(a, summed, x_in, back, ret):
        def body(c):
            x_out(a, c).wait_recv()
            total = (summed[c, pl.ds(0, rows), :] + x_in[c].astype(F32)).astype(BF)
            back[c, pl.ds(0, cap), :] = total[:cap]
            ret[c] = total[cap:]
            for copy in going_back(a, c):
                copy.start()

        return body

    each_chunk(near_step(0, sum_f, x_f, back_f, ret_f))
    near_b = near_step(1, sum_b, x_b, back_b, ret_b)

    def final_f(c):
        for copy in going_back(0, c):
            copy.wait_recv()
        values = dot(st_f[...], back_f[c])
        fin_f[c] = (fx[:, col(c)].astype(F32) + fw[...] * values).astype(BF)
        leaving(0, c).start()

    def near_b_final_f(c):
        near_b(c)
        final_f(c)

    each_chunk(near_b_final_f)

    def gather_b(c, carry):
        for copy in going_back(1, c):
            copy.wait_recv()
        unit_grad = gain[:, col(c)] * dot(st_b[...], back_b[c])
        ngr[c] = unit_grad
        unit = bx[:, col(c)].astype(F32) * scale_b[...]
        return carry + jnp.sum(unit_grad * unit, axis=-1, keepdims=True)

    mean = lax.fori_loop(0, chunks, gather_b, jnp.zeros((tokens, 1), F32)) / width

    def final_b(c):
        unit = bx[:, col(c)].astype(F32) * scale_b[...]
        grad = og[:, col(c)].astype(F32) + scale_b[...] * (ngr[c] - unit * mean)
        fin_b[c] = grad.astype(BF)
        leaving(1, c).start()

    each_chunk(final_b)

    for copy in pending:
        copy.wait_send()

    def drain(c):
        down_chunk(c).wait_send()
        for a in range(2):
            x_out(a, c).wait_send()
            for copy in going_back(a, c):
                copy.wait_send()
            leaving(a, c).wait()

    each_chunk(drain)


def fused(fi, fr, fwt, bi, br, bwt, og, gain, gate, up, down, experts, group, cap):
    tokens, width = fi.shape
    hd = gate.shape[1]
    rows = experts * cap
    cw = 512
    chunks = width // cw
    vm = pltpu.VMEM
    sem = pltpu.SemaphoreType.DMA
    others = experts - 1
    scratch = [vm((width, hd), BF)] * 4 + [vm((2 * hd, width), BF)]
    scratch += [vm((2 * rows, width), BF)] * 3 + [vm((others * cap, width), BF)] * 3
    scratch += [vm((2 * rows, hd), F32)] * 3 + [vm((2 * rows, 2 * hd), BF)] * 3
    scratch += [vm((chunks, rows, cw), BF)] * 6 + [vm((chunks, others * cap, cw), BF)] * 2
    scratch += [vm((chunks, tokens, cw), F32)] + [vm((chunks, tokens, cw), BF)] * 2
    scratch += [vm((tokens, width), BF), vm((tokens, 1), F32)]
    scratch += [vm((rows, tokens), BF)] * 2 + [vm((tokens, rows), BF)] * 2
    scratch += [vm((chunks, 2 * rows, cw), F32)] * 2
    scratch += [sem((2, 2)), sem((chunks,)), sem((chunks,)), sem((3,)), sem((3, others)), sem((3, others))]
    scratch += [sem((3,))] * 4 + [sem((2, chunks))] * 2
    scratch += [sem((2, chunks, others))] * 2 + [sem((2, chunks))] * 2
    out = jax.ShapeDtypeStruct((tokens, width), BF)
    anywhere = pl.BlockSpec(memory_space=pl.ANY)
    return pl.pallas_call(
        functools.partial(section_kernel, (experts, group, cap, chunks, cw)),
        out_shape=(out, out),
        in_specs=[pl.BlockSpec(memory_space=vm)] * 10 + [anywhere] * 3,
        out_specs=(anywhere, anywhere),
        scratch_shapes=scratch,
        compiler_params=pltpu.CompilerParams(
            collective_id=0, has_side_effects=True, vmem_limit_bytes=58 * 1024 * 1024
        ),
    )(fi, bi, og, gain, fwt, bwt, fr, fr.T, br, br.T, gate, up, down)


def per_device(
    forward_input,
    forward_route,
    forward_weight,
    backward_input,
    backward_route,
    backward_weight,
    output_grad,
    norm_gain,
    gate_weight,
    up_weight,
    down_weight,
):
    group = HID // gate_weight.shape[2]
    assert group == 4
    experts = lax.axis_size("expert") // group
    tokens = forward_input.shape[1]
    top = forward_route.shape[2]
    width = forward_input.shape[2]
    capacity = max(2, 3 * tokens * top // (2 * experts))
    if top == 1 and capacity % 16 == 0 and tokens % 16 == 0 and width % 512 == 0:
        next_input, previous_grad = fused(
            forward_input[0], forward_route[0], forward_weight[0],
            backward_input[0], backward_route[0], backward_weight[0],
            output_grad[0], norm_gain, gate_weight[0], up_weight[0], down_weight[0],
            experts, group, capacity,
        )
        return (next_input[None], previous_grad[None])
    mine = lax.axis_index("expert") // group
    gain = norm_gain[0]
    own = (gate_weight[0], up_weight[0], down_weight[0])
    other = tuple(swapped(w, 2) for w in own)
    weights = (own, other)

    ahead_wide, ahead_scale, ahead_normed = normalize(forward_input[0], gain)
    behind_wide, behind_scale, behind_normed = normalize(backward_input[0], gain)
    cotangent = output_grad[0].astype(jnp.float32)
    routed_grad = (
        jnp.repeat(cotangent, top, axis=0) * backward_weight[0].reshape(-1)[:, None]
    ).astype(jnp.bfloat16)
    ahead_slots = slot_matrix(forward_route[0], experts, capacity, mine)
    behind_slots = slot_matrix(backward_route[0], experts, capacity, mine)

    def gathered(matrix, rows):
        pieces = across(to_slots(matrix, rows), experts, group, 1)
        near = jnp.concatenate(pieces, axis=0)
        far = jnp.concatenate(
            [swapped(pieces[0], 1), swapped(jnp.concatenate(pieces[1:], axis=0), 1)], axis=0
        )
        return near, far

    def returned(near_sum, far_sum):
        total = (near_sum + swapped(far_sum.astype(jnp.bfloat16), 1)).astype(jnp.bfloat16)
        return jnp.concatenate(across(total, experts, group, -1), axis=0)

    ahead_near, ahead_far = gathered(ahead_slots, jnp.repeat(ahead_normed, top, axis=0))
    behind_near, behind_far = gathered(behind_slots, jnp.repeat(behind_normed, top, axis=0))
    grad_near, grad_far = gathered(behind_slots, routed_grad)

    ahead_back = returned(forward_sum(ahead_near, weights), forward_sum(ahead_far, weights))
    ahead_values = from_slots(ahead_slots, ahead_back)
    mixed = jnp.sum(
        ahead_values.reshape(tokens, top, width) * forward_weight[0][:, :, None], axis=1
    )
    section_out = (ahead_wide + mixed).astype(jnp.bfloat16)
    next_input = passed_along(section_out, "pipe", 1)

    behind_back = returned(
        backward_sum(behind_near, grad_near, weights), backward_sum(behind_far, grad_far, weights)
    )
    behind_values = from_slots(behind_slots, behind_back)
    normed_grad = jnp.sum(behind_values.reshape(tokens, top, width), axis=1)
    unit = behind_wide * behind_scale
    unit_grad = gain * normed_grad
    section_grad = cotangent + behind_scale * (
        unit_grad - unit * jnp.mean(unit_grad * unit, axis=-1, keepdims=True)
    )
    section_grad = section_grad.astype(jnp.bfloat16)
    previous_grad = passed_along(section_grad, "pipe", -1)
    return (next_input[None], previous_grad[None])


def solution(mesh):
    return jax.shard_map(
        per_device,
        mesh=mesh,
        in_specs=(
            P("pipe", "expert", None),
            P("pipe", "expert", None),
            P("pipe", "expert", None),
            P("pipe", "expert", None),
            P("pipe", "expert", None),
            P("pipe", "expert", None),
            P("pipe", "expert", None),
            P("pipe", None),
            P("pipe", None, "expert"),
            P("pipe", None, "expert"),
            P("pipe", "expert", None),
        ),
        out_specs=(P("pipe", "expert", None), P("pipe", "expert", None)),
        check_vma=False,
    )
```

```python
import functools

import jax
import jax.numpy as jnp
from jax import lax
from jax.experimental import pallas as pl
from jax.experimental.pallas import tpu as pltpu
from jax.sharding import PartitionSpec as P

HID = 1024


EPS = 1e-06


def passed_along(array, axis, by):
    devices = lax.axis_size(axis)
    return lax.ppermute(array, axis, [(i, (i + by) % devices) for i in range(devices)])


def swapped(array, bit):
    devices = lax.axis_size("expert")
    return lax.ppermute(array, "expert", [(i, i ^ bit) for i in range(devices)])


def normalize(values, gain):
    widened = values.astype(jnp.float32)
    scale = lax.rsqrt(jnp.mean(widened * widened, axis=-1, keepdims=True) + EPS)
    return (widened, scale, (widened * scale * gain).astype(jnp.bfloat16))


def slot_matrix(routes, experts, capacity, mine):
    flat = lax.rem(routes.reshape(-1) + (experts - mine), experts)
    pairs = flat.shape[0]
    onehot = flat[:, None] == jnp.arange(experts, dtype=jnp.int32)[None, :]
    before = jnp.arange(pairs)[:, None] > jnp.arange(pairs)[None, :]
    counts = jnp.dot(
        before.astype(jnp.bfloat16), onehot.astype(jnp.bfloat16), preferred_element_type=jnp.float32
    )
    ranks = jnp.sum(jnp.where(onehot, counts, 0.0), axis=1).astype(jnp.int32)
    target = flat * capacity + ranks
    slots = jnp.arange(experts * capacity, dtype=jnp.int32)
    return (slots[:, None] == target[None, :]).astype(jnp.bfloat16)


def to_slots(matrix, rows):
    return jnp.dot(matrix, rows, preferred_element_type=jnp.float32).astype(jnp.bfloat16)


def from_slots(matrix, rows):
    return lax.dot_general(
        matrix, rows, (((0,), (0,)), ((), ())), preferred_element_type=jnp.float32
    )


def across(slots, experts, group, sign):
    blocks = jnp.split(slots, experts, axis=0)
    return blocks[:1] + [
        passed_along(blocks[k], "expert", sign * group * k) for k in range(1, experts)
    ]


def dot(a, b):
    return jnp.dot(a, b, preferred_element_type=jnp.float32)


def dot_t(a, b):
    return lax.dot_general(a, b, (((1,), (1,)), ((), ())), preferred_element_type=jnp.float32)


def forward_sum(rows, weights):
    total = None
    for gate, up, down in weights:
        hidden = (jax.nn.silu(dot(rows, gate)) * dot(rows, up)).astype(jnp.bfloat16)
        part = dot(hidden, down)
        total = part if total is None else total + part
    return total


def backward_sum(rows, grads, weights):
    total = None
    for gate, up, down in weights:
        gate_back = dot(rows, gate)
        up_back = dot(rows, up)
        hidden_grad = dot_t(grads, down)
        sig = jax.nn.sigmoid(gate_back)
        gate_grad = (hidden_grad * up_back * sig * (1.0 + gate_back * (1.0 - sig))).astype(
            jnp.bfloat16
        )
        up_grad = (hidden_grad * gate_back * sig).astype(jnp.bfloat16)
        part = dot_t(gate_grad, gate) + dot_t(up_grad, up)
        total = part if total is None else total + part
    return total


MESH = pl.DeviceIdType.MESH
BF = jnp.bfloat16
F32 = jnp.float32


def slot_masks(row, scale_row, experts, cap, mine):
    def relative(route):
        return jnp.where(route >= mine, route - mine, route - mine + experts).astype(F32)

    tokens, rows = row.shape[1], experts * cap
    rel_r = relative(row)
    first = lax.broadcasted_iota(jnp.int32, (tokens, tokens), 0)
    second = lax.broadcasted_iota(jnp.int32, (tokens, tokens), 1)

    def upright(values):
        return jnp.sum(jnp.where(first == second, values, 0.0), axis=1, keepdims=True)

    rel_c = upright(rel_r)
    same = jnp.where(rel_c == rel_r, 1.0, 0.0)
    rank_c = jnp.sum(jnp.where(first > second, same, 0.0), axis=1, keepdims=True)
    rank_r = jnp.sum(jnp.where(first < second, same, 0.0), axis=0, keepdims=True)
    down = lax.broadcasted_iota(jnp.int32, (rows, tokens), 0).astype(F32)
    along = lax.broadcasted_iota(jnp.int32, (tokens, rows), 1).astype(F32)
    to_slot = jnp.where(down == rel_r * cap + rank_r, 1.0, 0.0).astype(BF)
    from_slot = jnp.where(along == rel_c * cap + rank_c, 1.0, 0.0).astype(BF)
    return to_slot, from_slot, upright(scale_row)


def section_kernel(
    cfg,
    fx, bx, og, gain, fw_r, bw_r, fr_r, br_r, gate, up, down,
    next_ref, prev_ref,
    g0, u0, g1, u1, dd, rows_f, rows_b, rows_g, out_f, out_b, out_g,
    acc_a, acc_b, acc_c, hid, ggr, ugr, far_f, far_b, x_f, x_b, back_f, back_b,
    ret_f, ret_b, ngr, fin_f, fin_b, tmp, scale_b, s_f, s_b, st_f, st_b, sum_f, sum_b, fw, bw,
    w_s, w_r, d_s, d_r, wl_sem, in_s, in_r, xl_s, xl_r, xf_s, xf_r, xo_s, xo_r, re_s, re_r, pi_s, pi_r,
):
    experts, group, cap, chunks, cw = cfg
    tokens, width = fx.shape
    rows = experts * cap
    hd = gate.shape[1]
    n = experts * group
    me = lax.axis_index("expert")
    pipe = lax.axis_index("pipe")
    pipes = lax.axis_size("pipe")
    xp = me + 1 - 2 * lax.rem(me, 2)
    zp = me + 2 - 4 * lax.rem(lax.div(me, 2), 2)
    onward = {"pipe": lax.rem(pipe + 1, pipes)}
    behind = {"pipe": lax.rem(pipe + pipes - 1, pipes)}

    def ahead_of(k):
        return {"expert": lax.rem(me + group * k, n)}

    def back_of(k):
        return {"expert": lax.rem(me + n - group * k, n)}

    def remote(src, dst, ss, rs, dev):
        return pltpu.make_async_remote_copy(
            src_ref=src, dst_ref=dst, send_sem=ss, recv_sem=rs, device_id=dev, device_id_type=MESH
        )

    barrier = pltpu.get_barrier_semaphore()
    peers = [ahead_of(k) for k in range(1, experts)]
    peers += [{"expert": xp}, {"expert": zp}, onward, behind]
    for peer in peers:
        pl.semaphore_signal(barrier, inc=1, device_id=peer, device_id_type=MESH)
    pl.semaphore_wait(barrier, len(peers))

    local = [
        pltpu.make_async_copy(src, dst, wl_sem.at[i])
        for i, (src, dst) in enumerate(((gate, g0), (up, u0), (down, dd.at[pl.ds(0, hd)])))
    ]

    def col(c):
        return pl.ds(pl.multiple_of(c * cw, cw), cw)

    def each_chunk(body):
        def step(c, carry):
            body(c)
            return carry

        lax.fori_loop(0, chunks, step, 0)

    def thick_chunk(kind, c):
        src, dst = ((gate, g1), (up, u1))[kind]
        return remote(
            src.at[col(c)], dst.at[col(c)], w_s.at[kind, c], w_r.at[kind, c], {"expert": zp}
        )

    def down_chunk(c):
        return remote(
            down.at[:, col(c)], dd.at[pl.ds(hd, hd), col(c)], d_s.at[c], d_r.at[c], {"expert": zp}
        )

    thick = [(kind, c) for c in range(chunks) for kind in range(2)]

    def send_weights(count):
        for kind, c in thick[:count]:
            thick_chunk(kind, c).start()
        del thick[:count]

    send_weights(2)
    for copy in local:
        copy.start()
    send_weights(1)

    def each_band(body):
        def step(i, carry):
            body(pl.ds(pl.multiple_of(i * 16, 16), 16))
            return carry

        lax.fori_loop(0, tokens // 16, step, 0)

    def norm_into(src, keep):
        def body(band):
            wide = src[band, :].astype(F32)
            scale = lax.rsqrt(jnp.mean(wide * wide, axis=-1, keepdims=True) + EPS)
            tmp[band, :] = (wide * scale * gain[...]).astype(BF)
            if keep is not None:
                keep[band, :] = scale

        each_band(body)

    def weigh_into():
        def body(band):
            tmp[band, :] = (og[band, :].astype(F32) * bw[band, :]).astype(BF)

        each_band(body)

    half = cap // 2

    def crossing(a, out, into):
        return [
            remote(
                out.at[pl.ds((k - 1) * cap + i * half, half)],
                into.at[pl.ds(k * cap + i * half, half)],
                in_s.at[a, k - 1, i],
                in_r.at[a, k - 1, i],
                ahead_of(k),
            )
            for i in range(2)
            for k in range(1, experts)
        ]

    def to_x(a, into, start, size, i, ss, rs):
        return remote(
            into.at[pl.ds(start, size)],
            into.at[pl.ds(rows + start, size)],
            ss.at[a, i],
            rs.at[a, i],
            {"expert": xp},
        )

    def near_x(a, into):
        return [to_x(a, into, i * half, half, i, xl_s, xl_r) for i in range(2)]

    def far_x(a, into):
        size = (rows - cap) // 2
        return [to_x(a, into, cap + i * size, size, i, xf_s, xf_r) for i in range(2)]

    def place(matrix, out, into):
        def body(c):
            picked = dot(matrix[...], tmp[:, col(c)]).astype(BF)
            into[pl.ds(0, cap), col(c)] = picked[:cap]
            out[:, col(c)] = picked[cap:]

        each_chunk(body)

    mine = lax.div(me, group)
    s_f[...], st_f[...], fw[...] = slot_masks(fr_r[...], fw_r[...], experts, cap, mine)
    s_b[...], st_b[...], bw[...] = slot_masks(br_r[...], bw_r[...], experts, cap, mine)
    sets = ((s_f, out_f, rows_f), (s_b, out_b, rows_b), (s_b, out_g, rows_g))
    pending = []
    crossings, nears, fars = [], [], []
    for a, (matrix, out, into) in enumerate(sets):
        if a == 0:
            norm_into(fx, None)
        elif a == 1:
            norm_into(bx, scale_b)
        else:
            weigh_into()
        place(matrix, out, into)
        cross = crossing(a, out, into)
        near = near_x(a, into)
        for i in range(2):
            for copy in cross[i * (experts - 1) : (i + 1) * (experts - 1)]:
                copy.start()
            near[i].start()
            send_weights(1)
        crossings.append(cross)
        nears.append(near)
        pending += cross + near

    for a in range(3):
        for copy in crossings[a]:
            copy.wait_recv()
        far = far_x(a, sets[a][2])
        for copy in far:
            copy.start()
            send_weights(1)
        fars.append(far)
        pending += far
    send_weights(len(thick))
    early = min(3, chunks)
    for c in range(early):
        down_chunk(c).start()
    for copy in local:
        copy.wait()

    def first(source, weight, acc):
        acc[...] = jnp.zeros_like(acc)

        def body(c):
            acc[...] += dot(source[:, col(c)], weight[col(c), :])

        each_chunk(body)

    def add_t(half, c):
        acc_c[...] += dot_t(rows_g[:, col(c)], dd[pl.ds(half * hd, hd), col(c)])

    def hidden_half(half, gw, uw):
        first(rows_f, gw, acc_a)
        first(rows_f, uw, acc_b)
        pre = acc_a[...]
        hid[:, pl.ds(half * hd, hd)] = (pre * jax.nn.sigmoid(pre) * acc_b[...]).astype(BF)

    def grads_start(gw, uw):
        first(rows_b, gw, acc_a)
        first(rows_b, uw, acc_b)
        acc_c[...] = jnp.zeros_like(acc_c)

    def grads_end(half):
        pre, upb, hg = acc_a[...], acc_b[...], acc_c[...]
        sig = jax.nn.sigmoid(pre)
        ggr[:, pl.ds(half * hd, hd)] = (hg * upb * sig * (1.0 + pre * (1.0 - sig))).astype(BF)
        ugr[:, pl.ds(half * hd, hd)] = (hg * pre * sig).astype(BF)

    for copy in nears[0] + fars[0]:
        copy.wait_recv()
    hidden_half(0, g0, u0)

    def own_f(c):
        sum_f[c] = dot(hid[:, pl.ds(0, hd)], dd[pl.ds(0, hd), col(c)])

    each_chunk(own_f)
    for a in (1, 2):
        for copy in nears[a] + fars[a]:
            copy.wait_recv()
    grads_start(g0, u0)
    each_chunk(functools.partial(add_t, 0))
    grads_end(0)

    def own_b(c):
        part = dot_t(ggr[:, pl.ds(0, hd)], g0[col(c), :])
        sum_b[c] = part + dot_t(ugr[:, pl.ds(0, hd)], u0[col(c), :])

    each_chunk(own_b)

    def thick_in(c):
        for kind in range(2):
            thick_chunk(kind, c).wait_recv()

    each_chunk(thick_in)
    hidden_half(1, g1, u1)
    grads_start(g1, u1)

    def x_out(a, c):
        src, dst = ((far_f, x_f), (far_b, x_b))[a]
        return remote(src.at[c], dst.at[c], xo_s.at[a, c], xo_r.at[a, c], {"expert": xp})

    def going_back(a, c):
        src, dst = ((ret_f, back_f), (ret_b, back_b))[a]
        return [
            remote(
                src.at[c, pl.ds((k - 1) * cap, cap)],
                dst.at[c, pl.ds(k * cap, cap)],
                re_s.at[a, c, k - 1],
                re_r.at[a, c, k - 1],
                back_of(k),
            )
            for k in range(1, experts)
        ]

    def leaving(a, c):
        src, dst, dev = ((fin_f, next_ref, onward), (fin_b, prev_ref, behind))[a]
        return remote(src.at[c], dst.at[:, col(c)], pi_s.at[a, c], pi_r.at[a, c], dev)

    def far_step_f(c):
        down_chunk(c).wait_recv()
        total = sum_f[c] + dot(hid[:, pl.ds(hd, hd)], dd[pl.ds(hd, hd), col(c)])
        far_f[c] = total[rows:].astype(BF)
        x_out(0, c).start()
        sum_f[c, pl.ds(0, rows), :] = total[:rows]
        add_t(1, c)

    def far_step_ahead(c, carry):
        far_step_f(c)
        down_chunk(c + early).start()
        return carry

    def far_step_last(c, carry):
        far_step_f(c)
        return carry

    lax.fori_loop(0, chunks - early, far_step_ahead, 0)
    lax.fori_loop(chunks - early, chunks, far_step_last, 0)
    grads_end(1)

    def far_step_b(c):
        total = sum_b[c] + dot_t(ggr[:, pl.ds(hd, hd)], g1[col(c), :])
        total = total + dot_t(ugr[:, pl.ds(hd, hd)], u1[col(c), :])
        far_b[c] = total[rows:].astype(BF)
        x_out(1, c).start()
        sum_b[c, pl.ds(0, rows), :] = total[:rows]

    each_chunk(far_step_b)

    def near_step(a, summed, x_in, back, ret):
        def body(c):
            x_out(a, c).wait_recv()
            total = (summed[c, pl.ds(0, rows), :] + x_in[c].astype(F32)).astype(BF)
            back[c, pl.ds(0, cap), :] = total[:cap]
            ret[c] = total[cap:]
            for copy in going_back(a, c):
                copy.start()

        return body

    each_chunk(near_step(0, sum_f, x_f, back_f, ret_f))
    near_b = near_step(1, sum_b, x_b, back_b, ret_b)

    def final_f(c):
        for copy in going_back(0, c):
            copy.wait_recv()
        values = dot(st_f[...], back_f[c])
        fin_f[c] = (fx[:, col(c)].astype(F32) + fw[...] * values).astype(BF)
        leaving(0, c).start()

    def near_b_final_f(c):
        near_b(c)
        final_f(c)

    each_chunk(near_b_final_f)

    def gather_b(c, carry):
        for copy in going_back(1, c):
            copy.wait_recv()
        unit_grad = gain[:, col(c)] * dot(st_b[...], back_b[c])
        ngr[c] = unit_grad
        unit = bx[:, col(c)].astype(F32) * scale_b[...]
        return carry + jnp.sum(unit_grad * unit, axis=-1, keepdims=True)

    mean = lax.fori_loop(0, chunks, gather_b, jnp.zeros((tokens, 1), F32)) / width

    def final_b(c):
        unit = bx[:, col(c)].astype(F32) * scale_b[...]
        grad = og[:, col(c)].astype(F32) + scale_b[...] * (ngr[c] - unit * mean)
        fin_b[c] = grad.astype(BF)
        leaving(1, c).start()

    each_chunk(final_b)

    for copy in pending:
        copy.wait_send()

    def drain(c):
        down_chunk(c).wait_send()
        for kind in range(2):
            thick_chunk(kind, c).wait_send()
        for a in range(2):
            x_out(a, c).wait_send()
            for copy in going_back(a, c):
                copy.wait_send()
            leaving(a, c).wait()

    each_chunk(drain)


def fused(fi, fr, fwt, bi, br, bwt, og, gain, gate, up, down, experts, group, cap):
    tokens, width = fi.shape
    hd = gate.shape[1]
    rows = experts * cap
    cw = 512
    chunks = width // cw
    vm = pltpu.VMEM
    sem = pltpu.SemaphoreType.DMA
    others = experts - 1
    scratch = [vm((width, hd), BF)] * 4 + [vm((2 * hd, width), BF)]
    scratch += [vm((2 * rows, width), BF)] * 3 + [vm((others * cap, width), BF)] * 3
    scratch += [vm((2 * rows, hd), F32)] * 3 + [vm((2 * rows, 2 * hd), BF)] * 3
    scratch += [vm((chunks, rows, cw), BF)] * 6 + [vm((chunks, others * cap, cw), BF)] * 2
    scratch += [vm((chunks, tokens, cw), F32)] + [vm((chunks, tokens, cw), BF)] * 2
    scratch += [vm((tokens, width), BF), vm((tokens, 1), F32)]
    scratch += [vm((rows, tokens), BF)] * 2 + [vm((tokens, rows), BF)] * 2
    scratch += [vm((chunks, 2 * rows, cw), F32)] * 2 + [vm((tokens, 1), F32)] * 2
    scratch += [sem((2, chunks))] * 2 + [sem((chunks,)), sem((chunks,)), sem((3,))]
    scratch += [sem((3, others, 2))] * 2
    scratch += [sem((3, 2))] * 4 + [sem((2, chunks))] * 2
    scratch += [sem((2, chunks, others))] * 2 + [sem((2, chunks))] * 2
    out = jax.ShapeDtypeStruct((tokens, width), BF)
    anywhere = pl.BlockSpec(memory_space=pl.ANY)
    return pl.pallas_call(
        functools.partial(section_kernel, (experts, group, cap, chunks, cw)),
        out_shape=(out, out),
        in_specs=[pl.BlockSpec(memory_space=vm)] * 8 + [anywhere] * 3,
        out_specs=(anywhere, anywhere),
        scratch_shapes=scratch,
        compiler_params=pltpu.CompilerParams(
            collective_id=0, has_side_effects=True, vmem_limit_bytes=58 * 1024 * 1024
        ),
    )(fi, bi, og, gain, *[v.reshape(1, tokens) for v in (fwt, bwt, fr, br)], gate, up, down)


def per_device(
    forward_input,
    forward_route,
    forward_weight,
    backward_input,
    backward_route,
    backward_weight,
    output_grad,
    norm_gain,
    gate_weight,
    up_weight,
    down_weight,
):
    group = HID // gate_weight.shape[2]
    assert group == 4
    experts = lax.axis_size("expert") // group
    tokens = forward_input.shape[1]
    top = forward_route.shape[2]
    width = forward_input.shape[2]
    capacity = max(2, 3 * tokens * top // (2 * experts))
    if top == 1 and capacity % 32 == 0 and tokens % 16 == 0 and width % 512 == 0:
        next_input, previous_grad = fused(
            forward_input[0], forward_route[0], forward_weight[0],
            backward_input[0], backward_route[0], backward_weight[0],
            output_grad[0], norm_gain, gate_weight[0], up_weight[0], down_weight[0],
            experts, group, capacity,
        )
        return (next_input[None], previous_grad[None])
    mine = lax.axis_index("expert") // group
    gain = norm_gain[0]
    own = (gate_weight[0], up_weight[0], down_weight[0])
    other = tuple(swapped(w, 2) for w in own)
    weights = (own, other)

    ahead_wide, ahead_scale, ahead_normed = normalize(forward_input[0], gain)
    behind_wide, behind_scale, behind_normed = normalize(backward_input[0], gain)
    cotangent = output_grad[0].astype(jnp.float32)
    routed_grad = (
        jnp.repeat(cotangent, top, axis=0) * backward_weight[0].reshape(-1)[:, None]
    ).astype(jnp.bfloat16)
    ahead_slots = slot_matrix(forward_route[0], experts, capacity, mine)
    behind_slots = slot_matrix(backward_route[0], experts, capacity, mine)

    def gathered(matrix, rows):
        pieces = across(to_slots(matrix, rows), experts, group, 1)
        near = jnp.concatenate(pieces, axis=0)
        far = jnp.concatenate(
            [swapped(pieces[0], 1), swapped(jnp.concatenate(pieces[1:], axis=0), 1)], axis=0
        )
        return near, far

    def returned(near_sum, far_sum):
        total = (near_sum + swapped(far_sum.astype(jnp.bfloat16), 1)).astype(jnp.bfloat16)
        return jnp.concatenate(across(total, experts, group, -1), axis=0)

    ahead_near, ahead_far = gathered(ahead_slots, jnp.repeat(ahead_normed, top, axis=0))
    behind_near, behind_far = gathered(behind_slots, jnp.repeat(behind_normed, top, axis=0))
    grad_near, grad_far = gathered(behind_slots, routed_grad)

    ahead_back = returned(forward_sum(ahead_near, weights), forward_sum(ahead_far, weights))
    ahead_values = from_slots(ahead_slots, ahead_back)
    mixed = jnp.sum(
        ahead_values.reshape(tokens, top, width) * forward_weight[0][:, :, None], axis=1
    )
    section_out = (ahead_wide + mixed).astype(jnp.bfloat16)
    next_input = passed_along(section_out, "pipe", 1)

    behind_back = returned(
        backward_sum(behind_near, grad_near, weights), backward_sum(behind_far, grad_far, weights)
    )
    behind_values = from_slots(behind_slots, behind_back)
    normed_grad = jnp.sum(behind_values.reshape(tokens, top, width), axis=1)
    unit = behind_wide * behind_scale
    unit_grad = gain * normed_grad
    section_grad = cotangent + behind_scale * (
        unit_grad - unit * jnp.mean(unit_grad * unit, axis=-1, keepdims=True)
    )
    section_grad = section_grad.astype(jnp.bfloat16)
    previous_grad = passed_along(section_grad, "pipe", -1)
    return (next_input[None], previous_grad[None])


def solution(mesh):
    return jax.shard_map(
        per_device,
        mesh=mesh,
        in_specs=(
            P("pipe", "expert", None),
            P("pipe", "expert", None),
            P("pipe", "expert", None),
            P("pipe", "expert", None),
            P("pipe", "expert", None),
            P("pipe", "expert", None),
            P("pipe", "expert", None),
            P("pipe", None),
            P("pipe", None, "expert"),
            P("pipe", None, "expert"),
            P("pipe", "expert", None),
        ),
        out_specs=(P("pipe", "expert", None), P("pipe", "expert", None)),
        check_vma=False,
    )
```

```python
import functools

import jax
import jax.numpy as jnp
from jax import lax
from jax.experimental import pallas as pl
from jax.experimental.pallas import tpu as pltpu
from jax.sharding import PartitionSpec as P

HID = 1024


EPS = 1e-06


def passed_along(array, axis, by):
    devices = lax.axis_size(axis)
    return lax.ppermute(array, axis, [(i, (i + by) % devices) for i in range(devices)])


def swapped(array, bit):
    devices = lax.axis_size("expert")
    return lax.ppermute(array, "expert", [(i, i ^ bit) for i in range(devices)])


def normalize(values, gain):
    widened = values.astype(jnp.float32)
    scale = lax.rsqrt(jnp.mean(widened * widened, axis=-1, keepdims=True) + EPS)
    return (widened, scale, (widened * scale * gain).astype(jnp.bfloat16))


def slot_matrix(routes, experts, capacity, mine):
    flat = lax.rem(routes.reshape(-1) + (experts - mine), experts)
    pairs = flat.shape[0]
    onehot = flat[:, None] == jnp.arange(experts, dtype=jnp.int32)[None, :]
    before = jnp.arange(pairs)[:, None] > jnp.arange(pairs)[None, :]
    counts = jnp.dot(
        before.astype(jnp.bfloat16), onehot.astype(jnp.bfloat16), preferred_element_type=jnp.float32
    )
    ranks = jnp.sum(jnp.where(onehot, counts, 0.0), axis=1).astype(jnp.int32)
    target = flat * capacity + ranks
    slots = jnp.arange(experts * capacity, dtype=jnp.int32)
    return (slots[:, None] == target[None, :]).astype(jnp.bfloat16)


def to_slots(matrix, rows):
    return jnp.dot(matrix, rows, preferred_element_type=jnp.float32).astype(jnp.bfloat16)


def from_slots(matrix, rows):
    return lax.dot_general(
        matrix, rows, (((0,), (0,)), ((), ())), preferred_element_type=jnp.float32
    )


def across(slots, experts, group, sign):
    blocks = jnp.split(slots, experts, axis=0)
    return blocks[:1] + [
        passed_along(blocks[k], "expert", sign * group * k) for k in range(1, experts)
    ]


def dot(a, b):
    return jnp.dot(a, b, preferred_element_type=jnp.float32)


def dot_t(a, b):
    return lax.dot_general(a, b, (((1,), (1,)), ((), ())), preferred_element_type=jnp.float32)


def forward_sum(rows, weights):
    total = None
    for gate, up, down in weights:
        hidden = (jax.nn.silu(dot(rows, gate)) * dot(rows, up)).astype(jnp.bfloat16)
        part = dot(hidden, down)
        total = part if total is None else total + part
    return total


def backward_sum(rows, grads, weights):
    total = None
    for gate, up, down in weights:
        gate_back = dot(rows, gate)
        up_back = dot(rows, up)
        hidden_grad = dot_t(grads, down)
        sig = jax.nn.sigmoid(gate_back)
        gate_grad = (hidden_grad * up_back * sig * (1.0 + gate_back * (1.0 - sig))).astype(
            jnp.bfloat16
        )
        up_grad = (hidden_grad * gate_back * sig).astype(jnp.bfloat16)
        part = dot_t(gate_grad, gate) + dot_t(up_grad, up)
        total = part if total is None else total + part
    return total


MESH = pl.DeviceIdType.MESH
BF = jnp.bfloat16
F32 = jnp.float32


def slot_masks(row, scale_row, experts, cap, mine):
    def relative(route):
        return jnp.where(route >= mine, route - mine, route - mine + experts).astype(F32)

    tokens, rows = row.shape[1], experts * cap
    rel_r = relative(row)
    first = lax.broadcasted_iota(jnp.int32, (tokens, tokens), 0)
    second = lax.broadcasted_iota(jnp.int32, (tokens, tokens), 1)

    def upright(values):
        return jnp.sum(jnp.where(first == second, values, 0.0), axis=1, keepdims=True)

    rel_c = upright(rel_r)
    same = jnp.where(rel_c == rel_r, 1.0, 0.0)
    rank_c = jnp.sum(jnp.where(first > second, same, 0.0), axis=1, keepdims=True)
    rank_r = jnp.sum(jnp.where(first < second, same, 0.0), axis=0, keepdims=True)
    down = lax.broadcasted_iota(jnp.int32, (rows, tokens), 0).astype(F32)
    along = lax.broadcasted_iota(jnp.int32, (tokens, rows), 1).astype(F32)
    to_slot = jnp.where(down == rel_r * cap + rank_r, 1.0, 0.0).astype(BF)
    from_slot = jnp.where(along == rel_c * cap + rank_c, 1.0, 0.0).astype(BF)
    return to_slot, from_slot, upright(scale_row)


def section_kernel(
    cfg,
    fx, bx, og, gain, fw_r, bw_r, fr_r, br_r, gate, up, down,
    next_ref, prev_ref,
    g0, u0, g1, u1, dd, rows_f, rows_b, rows_g, out_f, out_b, out_g,
    acc_a, acc_b, acc_c, hid, ggr, ugr, far_f, far_b, x_f, x_b, back_f, back_b,
    ret_f, ret_b, ngr, fin_f, fin_b, tmp, scale_b, s_f, s_b, st_f, st_b, sum_f, sum_b, fw, bw,
    w_s, w_r, d_s, d_r, wl_sem, in_s, in_r, xl_s, xl_r, xf_s, xf_r, xo_s, xo_r, re_s, re_r, pi_s, pi_r,
):
    experts, group, cap, chunks, cw = cfg
    tokens, width = fx.shape
    rows = experts * cap
    hd = gate.shape[1]
    n = experts * group
    me = lax.axis_index("expert")
    pipe = lax.axis_index("pipe")
    pipes = lax.axis_size("pipe")
    xp = me + 1 - 2 * lax.rem(me, 2)
    zp = me + 2 - 4 * lax.rem(lax.div(me, 2), 2)
    onward = {"pipe": lax.rem(pipe + 1, pipes)}
    behind = {"pipe": lax.rem(pipe + pipes - 1, pipes)}

    def ahead_of(k):
        return {"expert": lax.rem(me + group * k, n)}

    def back_of(k):
        return {"expert": lax.rem(me + n - group * k, n)}

    def remote(src, dst, ss, rs, dev):
        return pltpu.make_async_remote_copy(
            src_ref=src, dst_ref=dst, send_sem=ss, recv_sem=rs, device_id=dev, device_id_type=MESH
        )

    barrier = pltpu.get_barrier_semaphore()
    peers = [ahead_of(k) for k in range(1, experts)]
    peers += [{"expert": xp}, {"expert": zp}, onward, behind]
    for peer in peers:
        pl.semaphore_signal(barrier, inc=1, device_id=peer, device_id_type=MESH)
    pl.semaphore_wait(barrier, len(peers))

    local = [
        pltpu.make_async_copy(src, dst, wl_sem.at[i])
        for i, (src, dst) in enumerate(((gate, g0), (up, u0), (down, dd.at[pl.ds(0, hd)])))
    ]

    def col(c):
        return pl.ds(pl.multiple_of(c * cw, cw), cw)

    def each_chunk(body):
        def step(c, carry):
            body(c)
            return carry

        lax.fori_loop(0, chunks, step, 0)

    def thick_chunk(kind, c):
        src, dst = ((gate, g1), (up, u1))[kind]
        return remote(
            src.at[col(c)], dst.at[col(c)], w_s.at[kind, c], w_r.at[kind, c], {"expert": zp}
        )

    def down_chunk(c):
        return remote(
            down.at[:, col(c)], dd.at[pl.ds(hd, hd), col(c)], d_s.at[c], d_r.at[c], {"expert": zp}
        )

    thick = [(kind, c) for c in range(chunks) for kind in range(2)]

    def send_weights(count):
        for kind, c in thick[:count]:
            thick_chunk(kind, c).start()
        del thick[:count]

    send_weights(2)
    for copy in local:
        copy.start()
    send_weights(1)

    def each_band(body):
        def step(i, carry):
            body(pl.ds(pl.multiple_of(i * 16, 16), 16))
            return carry

        lax.fori_loop(0, tokens // 16, step, 0)

    def norm_into(src, keep):
        def body(band):
            wide = src[band, :].astype(F32)
            scale = lax.rsqrt(jnp.mean(wide * wide, axis=-1, keepdims=True) + EPS)
            tmp[band, :] = (wide * scale * gain[...]).astype(BF)
            if keep is not None:
                keep[band, :] = scale

        each_band(body)

    def weigh_into():
        def body(band):
            tmp[band, :] = (og[band, :].astype(F32) * bw[band, :]).astype(BF)

        each_band(body)

    half = cap // 2

    def crossing(a, out, into):
        return [
            remote(
                out.at[pl.ds((k - 1) * cap + i * half, half)],
                into.at[pl.ds(k * cap + i * half, half)],
                in_s.at[a, k - 1, i],
                in_r.at[a, k - 1, i],
                ahead_of(k),
            )
            for i in range(2)
            for k in range(1, experts)
        ]

    def to_x(a, into, start, size, i, ss, rs):
        return remote(
            into.at[pl.ds(start, size)],
            into.at[pl.ds(rows + start, size)],
            ss.at[a, i],
            rs.at[a, i],
            {"expert": xp},
        )

    def near_x(a, into):
        return [to_x(a, into, i * half, half, i, xl_s, xl_r) for i in range(2)]

    def far_x(a, into):
        size = (rows - cap) // 2
        return [to_x(a, into, cap + i * size, size, i, xf_s, xf_r) for i in range(2)]

    def place(matrix, out, into):
        def body(c):
            picked = dot(matrix[...], tmp[:, col(c)]).astype(BF)
            into[pl.ds(0, cap), col(c)] = picked[:cap]
            out[:, col(c)] = picked[cap:]

        each_chunk(body)

    mine = lax.div(me, group)
    s_f[...], st_f[...], fw[...] = slot_masks(fr_r[...], fw_r[...], experts, cap, mine)
    s_b[...], st_b[...], bw[...] = slot_masks(br_r[...], bw_r[...], experts, cap, mine)
    sets = ((s_f, out_f, rows_f), (s_b, out_b, rows_b), (s_b, out_g, rows_g))
    pending = []
    crossings, nears, fars = [], [], []
    for a, (matrix, out, into) in enumerate(sets):
        if a == 0:
            norm_into(fx, None)
        elif a == 1:
            norm_into(bx, scale_b)
        else:
            weigh_into()
        place(matrix, out, into)
        cross = crossing(a, out, into)
        near = near_x(a, into)
        for i in range(2):
            for copy in cross[i * (experts - 1) : (i + 1) * (experts - 1)]:
                copy.start()
            near[i].start()
            send_weights(1)
        crossings.append(cross)
        nears.append(near)
        pending += cross + near

    def first(source, weight, acc):
        acc[...] = jnp.zeros_like(acc)

        def body(c):
            acc[...] += dot(source[:, col(c)], weight[col(c), :])

        each_chunk(body)

    def add_t(half, c):
        acc_c[...] += dot_t(rows_g[:, col(c)], dd[pl.ds(half * hd, hd), col(c)])

    def hidden_half(half, gw, uw):
        first(rows_f, gw, acc_a)
        first(rows_f, uw, acc_b)
        pre = acc_a[...]
        hid[:, pl.ds(half * hd, hd)] = (pre * jax.nn.sigmoid(pre) * acc_b[...]).astype(BF)

    def grads_start(gw, uw):
        first(rows_b, gw, acc_a)
        first(rows_b, uw, acc_b)
        acc_c[...] = jnp.zeros_like(acc_c)

    def grads_end(half):
        pre, upb, hg = acc_a[...], acc_b[...], acc_c[...]
        sig = jax.nn.sigmoid(pre)
        ggr[:, pl.ds(half * hd, hd)] = (hg * upb * sig * (1.0 + pre * (1.0 - sig))).astype(BF)
        ugr[:, pl.ds(half * hd, hd)] = (hg * pre * sig).astype(BF)

    def forward_on(a):
        for copy in crossings[a]:
            copy.wait_recv()
        far = far_x(a, sets[a][2])
        for copy in far:
            copy.start()
            send_weights(1)
        fars.append(far)
        pending.extend(far)

    def all_in(a):
        for copy in nears[a] + fars[a]:
            copy.wait_recv()

    forward_on(0)
    for copy in local:
        copy.wait()
    forward_on(1)
    all_in(0)
    hidden_half(0, g0, u0)

    def own_f(c):
        sum_f[c] = dot(hid[:, pl.ds(0, hd)], dd[pl.ds(0, hd), col(c)])

    each_chunk(own_f)
    send_weights(1)
    all_in(1)
    grads_start(g0, u0)
    forward_on(2)
    send_weights(len(thick))
    early = min(5, chunks)
    for c in range(early):
        down_chunk(c).start()
    all_in(2)
    each_chunk(functools.partial(add_t, 0))
    grads_end(0)

    def own_b(c):
        part = dot_t(ggr[:, pl.ds(0, hd)], g0[col(c), :])
        sum_b[c] = part + dot_t(ugr[:, pl.ds(0, hd)], u0[col(c), :])

    each_chunk(own_b)

    def thick_in(c):
        for kind in range(2):
            thick_chunk(kind, c).wait_recv()

    each_chunk(thick_in)
    hidden_half(1, g1, u1)
    grads_start(g1, u1)

    def x_out(a, c):
        src, dst = ((far_f, x_f), (far_b, x_b))[a]
        return remote(src.at[c], dst.at[c], xo_s.at[a, c], xo_r.at[a, c], {"expert": xp})

    def going_back(a, c):
        src, dst = ((ret_f, back_f), (ret_b, back_b))[a]
        return [
            remote(
                src.at[c, pl.ds((k - 1) * cap, cap)],
                dst.at[c, pl.ds(k * cap, cap)],
                re_s.at[a, c, k - 1],
                re_r.at[a, c, k - 1],
                back_of(k),
            )
            for k in range(1, experts)
        ]

    def leaving(a, c):
        src, dst, dev = ((fin_f, next_ref, onward), (fin_b, prev_ref, behind))[a]
        return remote(src.at[c], dst.at[:, col(c)], pi_s.at[a, c], pi_r.at[a, c], dev)

    def far_step_f(c):
        down_chunk(c).wait_recv()
        total = sum_f[c] + dot(hid[:, pl.ds(hd, hd)], dd[pl.ds(hd, hd), col(c)])
        far_f[c] = total[rows:].astype(BF)
        x_out(0, c).start()
        sum_f[c, pl.ds(0, rows), :] = total[:rows]
        add_t(1, c)

    def far_step_ahead(c, carry):
        far_step_f(c)
        down_chunk(c + early).start()
        return carry

    def far_step_last(c, carry):
        far_step_f(c)
        return carry

    lax.fori_loop(0, chunks - early, far_step_ahead, 0)
    lax.fori_loop(chunks - early, chunks, far_step_last, 0)
    grads_end(1)

    def far_step_b(c):
        total = sum_b[c] + dot_t(ggr[:, pl.ds(hd, hd)], g1[col(c), :])
        total = total + dot_t(ugr[:, pl.ds(hd, hd)], u1[col(c), :])
        far_b[c] = total[rows:].astype(BF)
        x_out(1, c).start()
        sum_b[c, pl.ds(0, rows), :] = total[:rows]

    each_chunk(far_step_b)

    def near_step(a, summed, x_in, back, ret):
        def body(c):
            x_out(a, c).wait_recv()
            total = (summed[c, pl.ds(0, rows), :] + x_in[c].astype(F32)).astype(BF)
            back[c, pl.ds(0, cap), :] = total[:cap]
            ret[c] = total[cap:]
            for copy in going_back(a, c):
                copy.start()

        return body

    each_chunk(near_step(0, sum_f, x_f, back_f, ret_f))
    near_b = near_step(1, sum_b, x_b, back_b, ret_b)

    def final_f(c):
        for copy in going_back(0, c):
            copy.wait_recv()
        values = dot(st_f[...], back_f[c])
        fin_f[c] = (fx[:, col(c)].astype(F32) + fw[...] * values).astype(BF)
        leaving(0, c).start()

    def near_b_final_f(c):
        near_b(c)
        final_f(c)

    each_chunk(near_b_final_f)

    def gather_b(c, carry):
        for copy in going_back(1, c):
            copy.wait_recv()
        unit_grad = gain[:, col(c)] * dot(st_b[...], back_b[c])
        ngr[c] = unit_grad
        unit = bx[:, col(c)].astype(F32) * scale_b[...]
        return carry + jnp.sum(unit_grad * unit, axis=-1, keepdims=True)

    mean = lax.fori_loop(0, chunks, gather_b, jnp.zeros((tokens, 1), F32)) / width

    def final_b(c):
        unit = bx[:, col(c)].astype(F32) * scale_b[...]
        grad = og[:, col(c)].astype(F32) + scale_b[...] * (ngr[c] - unit * mean)
        fin_b[c] = grad.astype(BF)
        leaving(1, c).start()

    each_chunk(final_b)

    for copy in pending:
        copy.wait_send()

    def drain(c):
        down_chunk(c).wait_send()
        for kind in range(2):
            thick_chunk(kind, c).wait_send()
        for a in range(2):
            x_out(a, c).wait_send()
            for copy in going_back(a, c):
                copy.wait_send()
            leaving(a, c).wait()

    each_chunk(drain)


def fused(fi, fr, fwt, bi, br, bwt, og, gain, gate, up, down, experts, group, cap):
    tokens, width = fi.shape
    hd = gate.shape[1]
    rows = experts * cap
    cw = 512
    chunks = width // cw
    vm = pltpu.VMEM
    sem = pltpu.SemaphoreType.DMA
    others = experts - 1
    scratch = [vm((width, hd), BF)] * 4 + [vm((2 * hd, width), BF)]
    scratch += [vm((2 * rows, width), BF)] * 3 + [vm((others * cap, width), BF)] * 3
    scratch += [vm((2 * rows, hd), F32)] * 3 + [vm((2 * rows, 2 * hd), BF)] * 3
    scratch += [vm((chunks, rows, cw), BF)] * 6 + [vm((chunks, others * cap, cw), BF)] * 2
    scratch += [vm((chunks, tokens, cw), F32)] + [vm((chunks, tokens, cw), BF)] * 2
    scratch += [vm((tokens, width), BF), vm((tokens, 1), F32)]
    scratch += [vm((rows, tokens), BF)] * 2 + [vm((tokens, rows), BF)] * 2
    scratch += [vm((chunks, 2 * rows, cw), F32)] * 2 + [vm((tokens, 1), F32)] * 2
    scratch += [sem((2, chunks))] * 2 + [sem((chunks,)), sem((chunks,)), sem((3,))]
    scratch += [sem((3, others, 2))] * 2
    scratch += [sem((3, 2))] * 4 + [sem((2, chunks))] * 2
    scratch += [sem((2, chunks, others))] * 2 + [sem((2, chunks))] * 2
    out = jax.ShapeDtypeStruct((tokens, width), BF)
    anywhere = pl.BlockSpec(memory_space=pl.ANY)
    return pl.pallas_call(
        functools.partial(section_kernel, (experts, group, cap, chunks, cw)),
        out_shape=(out, out),
        in_specs=[pl.BlockSpec(memory_space=vm)] * 8 + [anywhere] * 3,
        out_specs=(anywhere, anywhere),
        scratch_shapes=scratch,
        compiler_params=pltpu.CompilerParams(
            collective_id=0, has_side_effects=True, vmem_limit_bytes=58 * 1024 * 1024
        ),
    )(fi, bi, og, gain, *[v.reshape(1, tokens) for v in (fwt, bwt, fr, br)], gate, up, down)


def per_device(
    forward_input,
    forward_route,
    forward_weight,
    backward_input,
    backward_route,
    backward_weight,
    output_grad,
    norm_gain,
    gate_weight,
    up_weight,
    down_weight,
):
    group = HID // gate_weight.shape[2]
    assert group == 4
    experts = lax.axis_size("expert") // group
    tokens = forward_input.shape[1]
    top = forward_route.shape[2]
    width = forward_input.shape[2]
    capacity = max(2, 3 * tokens * top // (2 * experts))
    if top == 1 and capacity % 32 == 0 and tokens % 16 == 0 and width % 512 == 0:
        next_input, previous_grad = fused(
            forward_input[0], forward_route[0], forward_weight[0],
            backward_input[0], backward_route[0], backward_weight[0],
            output_grad[0], norm_gain, gate_weight[0], up_weight[0], down_weight[0],
            experts, group, capacity,
        )
        return (next_input[None], previous_grad[None])
    mine = lax.axis_index("expert") // group
    gain = norm_gain[0]
    own = (gate_weight[0], up_weight[0], down_weight[0])
    other = tuple(swapped(w, 2) for w in own)
    weights = (own, other)

    ahead_wide, ahead_scale, ahead_normed = normalize(forward_input[0], gain)
    behind_wide, behind_scale, behind_normed = normalize(backward_input[0], gain)
    cotangent = output_grad[0].astype(jnp.float32)
    routed_grad = (
        jnp.repeat(cotangent, top, axis=0) * backward_weight[0].reshape(-1)[:, None]
    ).astype(jnp.bfloat16)
    ahead_slots = slot_matrix(forward_route[0], experts, capacity, mine)
    behind_slots = slot_matrix(backward_route[0], experts, capacity, mine)

    def gathered(matrix, rows):
        pieces = across(to_slots(matrix, rows), experts, group, 1)
        near = jnp.concatenate(pieces, axis=0)
        far = jnp.concatenate(
            [swapped(pieces[0], 1), swapped(jnp.concatenate(pieces[1:], axis=0), 1)], axis=0
        )
        return near, far

    def returned(near_sum, far_sum):
        total = (near_sum + swapped(far_sum.astype(jnp.bfloat16), 1)).astype(jnp.bfloat16)
        return jnp.concatenate(across(total, experts, group, -1), axis=0)

    ahead_near, ahead_far = gathered(ahead_slots, jnp.repeat(ahead_normed, top, axis=0))
    behind_near, behind_far = gathered(behind_slots, jnp.repeat(behind_normed, top, axis=0))
    grad_near, grad_far = gathered(behind_slots, routed_grad)

    ahead_back = returned(forward_sum(ahead_near, weights), forward_sum(ahead_far, weights))
    ahead_values = from_slots(ahead_slots, ahead_back)
    mixed = jnp.sum(
        ahead_values.reshape(tokens, top, width) * forward_weight[0][:, :, None], axis=1
    )
    section_out = (ahead_wide + mixed).astype(jnp.bfloat16)
    next_input = passed_along(section_out, "pipe", 1)

    behind_back = returned(
        backward_sum(behind_near, grad_near, weights), backward_sum(behind_far, grad_far, weights)
    )
    behind_values = from_slots(behind_slots, behind_back)
    normed_grad = jnp.sum(behind_values.reshape(tokens, top, width), axis=1)
    unit = behind_wide * behind_scale
    unit_grad = gain * normed_grad
    section_grad = cotangent + behind_scale * (
        unit_grad - unit * jnp.mean(unit_grad * unit, axis=-1, keepdims=True)
    )
    section_grad = section_grad.astype(jnp.bfloat16)
    previous_grad = passed_along(section_grad, "pipe", -1)
    return (next_input[None], previous_grad[None])


def solution(mesh):
    return jax.shard_map(
        per_device,
        mesh=mesh,
        in_specs=(
            P("pipe", "expert", None),
            P("pipe", "expert", None),
            P("pipe", "expert", None),
            P("pipe", "expert", None),
            P("pipe", "expert", None),
            P("pipe", "expert", None),
            P("pipe", "expert", None),
            P("pipe", None),
            P("pipe", None, "expert"),
            P("pipe", None, "expert"),
            P("pipe", "expert", None),
        ),
        out_specs=(P("pipe", "expert", None), P("pipe", "expert", None)),
        check_vma=False,
    )
```
